32 devices in a mesh: row: 8 (over y, x, core), col: 4 (over z).
Axes of the slice: x: 2, y: 2, z: 4, core: 2. Of those that a mesh axis runs over, the one named last changes fastest.
Arguments:
- nodes: bfloat16 [8192, 256], P(('row', 'col')), may hold values from -6 to 6
- weight: bfloat16 [256, 256], replicated, may hold values from -0.375 to 0.375
- adjacency: bfloat16 [8192, 8192], P('row', 'col'), may hold values from -0.09375 to 0.09375
- history: bfloat16 [32768, 256], P(('row', 'col')), may hold values from -6 to 6
- pull_owner: int32 [1024, 1], P(('row', 'col')), may hold values from 0 to 7; in each aligned block of 32 rows (0 to 31, 32 to 63, ...) at most 4 rows name the same one
- pull_slot: int32 [1024], P(('row', 'col')), may hold values from 0 to 7
- pull_target: int32 [1024], P(('row', 'col')), may hold values from 0 to 7
- hist_tiles: bfloat16 [1024, 128, 128], P(('row', 'col')), may hold values from -0.375 to 0.375
- cotangent: bfloat16 [8192, 256], P(('row', 'col')), may hold values from -6 to 6
Outputs:
- activated: bfloat16 [8192, 256], P(('row', 'col'))
- grad_nodes: bfloat16 [8192, 256], P(('row', 'col'))
- grad_weight: float32 [256, 256], replicated
The draws below stay inside these ranges and needn't reach their ends.
Inputs may be any that keep to these rules, and one draw needn't show every extreme that they name: `pull_owner`: among the 32 pulls of one device no owner is named more than 4 times, a bound that some block reaches.
All inputs are finite; a program needn't handle non-finite values.
Results may differ from the reference program's by a relative error of at most 0.029.
Values may be sent and summed in bfloat16 or wider, within the bound.
No kernel may reach another device: no remote copies, remote signals or barrier semaphores. Data moves between devices by JAX's collectives and lax.ppermute only.
A program may use at most 128 MiB of HBM per device.

```python
import math
import jax
import jax.numpy as jnp
import numpy as np
from jax import lax

HID = 256
BLK = 128
N_DEV = 256
K = 32
CAP = 4
HB_DEV = 8
NODES = 8192
N_ROW = 8
N_COL = 4
DEVICES = 32


def touch_ends(drawn, key, low, largest):
    longest = drawn.shape.index(max(drawn.shape))
    spots = []
    for shift in (0, 1):
        where = [jax.random.randint(jax.random.fold_in(key, axis), (), 0, length) for axis, length in enumerate(drawn.shape)]
        where[longest] = (where[longest] + shift) % drawn.shape[longest]
        spots.append(tuple(where))
    return drawn.at[spots[0]].set(low).at[spots[1]].set(largest)


def raised(array, key, source, target, blocks, factor):
    def block_of(position):
        return (jnp.arange(array.shape[position]) // (array.shape[position] // blocks)).reshape((-1,) + (1,) * (array.ndim - 1 - position))

    near = jax.random.permutation(key, blocks)[block_of(target)]
    far = (block_of(target) + blocks // 2) % blocks
    return jnp.where((block_of(source) == near) | (block_of(source) == far), factor * array, array)


def level_of(rng, extent, shards, least, high):
    def one(axis_at, parts):
        draws = jax.random.uniform(jax.random.fold_in(jax.random.fold_in(rng, 6), axis_at), (parts,), jnp.float32, least / len(shards), high / len(shards))
        return jnp.repeat(jnp.exp(draws), extent[axis_at] // parts).reshape((-1,) + (1,) * (len(extent) - axis_at - 1))

    level = one(*shards[0])
    for cut in shards[1:]:
        level = level * one(*cut)
    return level


def shared_out(key, own, number, rows, amount, top, most, slope):
    ranking = jax.random.permutation(key, amount)
    packed, ordinary = portions_of(amount, rows * top, most, slope, True), portions_of(amount, rows * top, most, slope, False)
    places = jnp.arange(amount)

    def named(lengths, offset_by):
        used = int((lengths > 0).sum())
        fixed = max(1, used // 4)
        passed = fixed + (places - fixed + offset_by * (used - fixed)) % max(1, amount - fixed)
        return jnp.zeros((amount,), jnp.int32).at[ranking[jnp.where(places < fixed, places, passed)]].set(jnp.asarray(lengths, jnp.int32))

    lengths = jnp.where(number % 4 == 0, named(packed, number // 4), named(ordinary, number - number // 4 - 1))
    mixed = jax.random.permutation(jax.random.fold_in(own, 3), amount)
    giver, taker = mixed[0:amount // 2 * 2:2], mixed[1:amount // 2 * 2:2]
    slack = jnp.minimum(lengths[giver] - 1, most - lengths[taker]) // 2
    slack = jnp.where((giver == ranking[0]) | (taker == ranking[0]) | (lengths[taker] == 0), 0, jnp.maximum(slack, 0))
    passed = jax.random.randint(jax.random.fold_in(own, 4), (amount // 2,), 0, 1 << 20) % (slack + 1)
    lengths = lengths.at[giver].add(-passed).at[taker].add(passed)
    items = jnp.searchsorted(jnp.cumsum(lengths), jnp.arange(rows * top), side="right").astype(jnp.int32)
    table = items.reshape(top, rows).T
    table = table[jax.random.permutation(jax.random.fold_in(own, 1), rows)]
    offset_by = jax.random.randint(jax.random.fold_in(own, 2), (rows, 1), 0, top)
    return jnp.take_along_axis(table, (jnp.arange(top)[None, :] + offset_by) % top, axis=1)


def portions_of(amount, total, reach, skew, full):
    portions = [(1 << 20) // math.isqrt(rank ** skew) + 1 for rank in range(1, amount + 1)]
    largest = reach if full else min(reach, max(-(-total // amount), total * portions[0] // sum(portions)))
    least = 1 if total - largest >= amount - 1 else 0
    holding, surplus = [largest] + [least] * (amount - 1), total - largest - least * (amount - 1)
    while surplus > 0:
        candidates = [i for i in range(1, amount) if holding[i] < largest] or [i for i in range(1, amount) if holding[i] < reach]
        pool, remaining = sum([portions[i] for i in candidates]), surplus
        for i in candidates:
            extra = min(reach - holding[i], max(1, remaining * portions[i] // pool), surplus)
            holding[i] = holding[i] + extra
            surplus = surplus - extra
    return np.array(holding)


def normal_values(own_key, extent, spread, bound, cuts=(), kind=jnp.bfloat16):
    factor_of = level_of(own_key, extent, cuts, -0.22, 0.18) if cuts else 1.0
    values = jax.random.normal(own_key, extent, jnp.float32) * spread * factor_of
    return jnp.minimum(jnp.maximum(values, -bound), bound).astype(kind)


def noise_with(own_key, dims, spread, limit, shards, heavy, held_as=jnp.bfloat16):
    values = spread * jax.random.normal(own_key, dims, jnp.float32)
    if shards:
        values = values * level_of(own_key, dims, shards, -0.22, 0.18)
    return jnp.clip(raised(values, jax.random.fold_in(own_key, 3), *heavy), -limit, limit).astype(held_as)


def setup_inputs(seed: int = 0) -> dict:
    arg_keys = jax.random.split(jax.random.key(seed), 10)
    nodes = normal_values(arg_keys[0], (NODES, HID), 1.0, 6.0, ((0, 32),))
    weight = normal_values(arg_keys[1], (HID, HID), HID ** -0.5, 0.375)
    adjacency = noise_with(arg_keys[2], (NODES, NODES), NODES ** -0.5, 0.09375, ((0, 8), (1, 4)), (1, 0, 8, 2.0))
    history = normal_values(arg_keys[3], (DEVICES * HB_DEV * BLK, HID), 1.0, 6.0, ((0, 32),))
    pull_owner_keys = jax.random.split(jax.random.fold_in(arg_keys[4], 1), (DEVICES * K) // K)
    pull_owner_turns = jax.random.permutation(jax.random.fold_in(arg_keys[4], 3), (DEVICES * K) // K)
    pull_owner = jax.vmap(lambda own, number: shared_out(jax.random.fold_in(arg_keys[4], 2), own, number, K, N_ROW, 1, CAP, 2))(pull_owner_keys, pull_owner_turns).reshape((DEVICES * K, 1))
    pull_slot = touch_ends(jax.random.randint(arg_keys[5], (DEVICES * K,), 0, HB_DEV), jax.random.fold_in(arg_keys[5], 1), 0, HB_DEV - 1).astype(jnp.int32)
    pull_target = touch_ends(jax.random.randint(arg_keys[6], (DEVICES * K,), 0, NODES // N_ROW // BLK), jax.random.fold_in(arg_keys[6], 1), 0, (NODES // N_ROW // BLK) - 1).astype(jnp.int32)
    hist_tiles = normal_values(arg_keys[7], (DEVICES * K, BLK, BLK), (2 * BLK) ** -0.5, 0.375, ((0, 32),))
    cotangent = normal_values(arg_keys[8], (NODES, HID), 1.0, 6.0, ((0, 32),))
    return {"nodes": nodes, "weight": weight, "adjacency": adjacency, "history": history, "pull_owner": pull_owner, "pull_slot": pull_slot, "pull_target": pull_target, "hist_tiles": hist_tiles, "cotangent": cotangent}


def reference(nodes, weight, adjacency, history, pull_owner, pull_slot, pull_target, hist_tiles, cotangent):
    projected = jnp.dot(nodes, weight, preferred_element_type=jnp.float32).astype(jnp.bfloat16)
    permuted = projected.reshape(N_ROW, N_COL, N_DEV, HID).transpose(1, 0, 2, 3).reshape(NODES, HID)
    panel_rows = NODES // N_ROW
    row_count = panel_rows // BLK
    blocks = history.reshape(N_ROW, N_COL, HB_DEV, BLK, HID)
    owners = pull_owner[:, 0].reshape(DEVICES, K)
    slot_ids = pull_slot.reshape(DEVICES, K)
    targets = pull_target.reshape(DEVICES, K)
    tiles_all = hist_tiles.reshape(DEVICES, K, BLK, BLK)

    def one_device(accum, device):
        row_index = device // N_COL
        col_index = device % N_COL
        fetched = blocks[owners[device], col_index, slot_ids[device]]
        products = jnp.einsum('kab,kbf->kaf', tiles_all[device].astype(jnp.float32), fetched.astype(jnp.float32), precision=lax.Precision.HIGHEST)
        placing = (targets[device][None, :] == jnp.arange(row_count, dtype=jnp.int32)[:, None]).astype(jnp.float32)
        term = jnp.einsum('jk,kaf->jaf', placing, products, precision=lax.Precision.HIGHEST).reshape(panel_rows, HID)
        begin = (row_index * panel_rows).astype(jnp.int32)
        current = lax.dynamic_slice_in_dim(accum, begin, panel_rows, 0)
        return (lax.dynamic_update_slice_in_dim(accum, current + term, begin, 0), None)
    history_term, _ = lax.scan(one_device, jnp.zeros((NODES, HID), jnp.float32), jnp.arange(DEVICES, dtype=jnp.int32))
    permuted_f = permuted.astype(jnp.float32)
    adjacency_panels = adjacency.reshape(N_ROW, panel_rows, NODES)

    def forward_panel(row_slab):
        return jnp.dot(row_slab.astype(jnp.float32), permuted_f, precision=lax.Precision.HIGHEST)
    mixed = lax.map(forward_panel, adjacency_panels).reshape(NODES, HID) + history_term
    activated = jax.nn.silu(mixed).astype(jnp.bfloat16)
    sigmoid_z = jax.nn.sigmoid(mixed)
    grad_pre = (cotangent.astype(jnp.float32) * sigmoid_z * (1.0 + mixed * (1.0 - sigmoid_z))).astype(jnp.bfloat16)
    grad_panels = grad_pre.reshape(N_ROW, panel_rows, HID)

    def backward_panel(accum, pieces):
        row_slab, grad_slab = pieces
        return (accum + jnp.dot(row_slab.astype(jnp.float32).T, grad_slab.astype(jnp.float32), precision=lax.Precision.HIGHEST), None)
    grad_perm, _ = lax.scan(backward_panel, jnp.zeros((NODES, HID), jnp.float32), (adjacency_panels, grad_panels))
    grad_proj = grad_perm.astype(jnp.bfloat16).reshape(N_COL, N_ROW, N_DEV, HID).transpose(1, 0, 2, 3).reshape(NODES, HID)
    grad_nodes = jnp.dot(grad_proj, weight.T, preferred_element_type=jnp.float32).astype(jnp.bfloat16)
    grad_weight = jnp.dot(nodes.astype(jnp.float32).T, grad_proj.astype(jnp.float32), precision=lax.Precision.HIGHEST) / math.sqrt(NODES)
    return (activated, grad_nodes, grad_weight)
```

```python
import functools
import math

import jax
import jax.numpy as jnp
from jax import lax
from jax.experimental import pallas as pl
from jax.experimental.pallas import tpu as pltpu
from jax.sharding import PartitionSpec as P

BLK = 128
CAP = 4
BF16 = jnp.bfloat16
F32 = jnp.float32
WHOLE = pl.BlockSpec(memory_space=pltpu.VMEM)
SCALARS = pl.BlockSpec(memory_space=pltpu.SMEM)


def swap(x, axis, offset):
    size = lax.axis_size(axis)
    return lax.ppermute(x, axis, [(i, i ^ offset) for i in range(size)])


def nbytes(*arrays):
    return sum(math.prod(a.shape) * jnp.dtype(a.dtype).itemsize for a in arrays)


def call(kernel, outs, scratch, flops, *operands, specs=None):
    held = nbytes(*operands, *outs) + nbytes(*scratch)
    return pl.pallas_call(
        kernel,
        out_shape=outs,
        in_specs=specs or [WHOLE] * len(operands),
        out_specs=[WHOLE] * len(outs),
        scratch_shapes=[pltpu.VMEM(s.shape, s.dtype) for s in scratch],
        compiler_params=pltpu.CompilerParams(vmem_limit_bytes=held + (8 << 20)),
        cost_estimate=pl.CostEstimate(flops=flops, bytes_accessed=held, transcendentals=0),
    )(*operands)


def aggregate_kernel(n_row, n_col, a_ref, *refs):
    pieces, outs, x_ref = refs[:n_row], refs[n_row:-1], refs[-1]
    span = pieces[0].shape[0]
    r, c = lax.axis_index("row"), lax.axis_index("col")
    for t in range(n_row):
        x_ref[pl.ds(pl.multiple_of((r ^ t) * span, span), span), :] = pieces[t][...]
    for s in range(n_col):
        rows = pl.ds(pl.multiple_of((c ^ s) * span, span), span)
        part = jnp.dot(a_ref[rows, :], x_ref[...], preferred_element_type=F32)
        outs[s][...] = part.astype(outs[s].dtype)


def history_kernel(n_row, n_col, which, slot, target, tiles, *refs):
    low, high = refs[:n_row], refs[n_row : 2 * n_row]
    outs, acc = refs[2 * n_row : -1], refs[-1]
    span = outs[0].shape[0]
    half = low[0].shape[0] // BLK
    c = lax.axis_index("col")
    acc[...] = jnp.zeros_like(acc)
    for t in range(n_row):
        for m in range(CAP):
            i = t * CAP + m
            at = slot[i]
            inside = pl.ds(pl.multiple_of((at % half) * BLK, BLK), BLK)
            block = jnp.where(at < half, low[t][inside, :], high[t][inside, :])
            rows = pl.ds(pl.multiple_of(target[i] * BLK, BLK), BLK)
            acc[rows, :] += jnp.dot(tiles[which[i]], block, preferred_element_type=F32)
    for s in range(n_col):
        rows = pl.ds(pl.multiple_of((c ^ s) * span, span), span)
        outs[s][...] = acc[rows, :].astype(outs[s].dtype)


def transposed_kernel(n_col, offsets, a_ref, *refs):
    pieces, outs, g_ref = refs[:n_col], refs[n_col:-1], refs[-1]
    span = pieces[0].shape[1]
    r, c = lax.axis_index("row"), lax.axis_index("col")
    for s in range(n_col):
        g_ref[:, pl.ds(pl.multiple_of((c ^ s) * span, span), span)] = pieces[s][...]
    for t, out in zip(offsets, outs, strict=True):
        columns = pl.ds(pl.multiple_of((r ^ t) * span, span), span)
        part = jnp.dot(g_ref[...], a_ref[:, columns], preferred_element_type=F32)
        out[...] = part.astype(out.dtype)


def spread_sum(x, axis, offsets):
    narrow = x.astype(BF16)
    terms = [(swap(narrow, axis, s) if s else narrow).astype(F32) for s in offsets]
    while len(terms) > 1:
        terms = [a + b for a, b in zip(terms[::2], terms[1::2], strict=True)]
    return terms[0]


def shape(*dims, dtype=BF16):
    return jax.ShapeDtypeStruct(dims, dtype)


def pull_lists(owner, slot, target, n_row, row_count):
    pulls = owner.shape[0]
    offset = owner ^ lax.axis_index("row")
    order = jnp.arange(pulls, dtype=jnp.int32)
    earlier = (offset[None, :] == offset[:, None]) & (order[None, :] < order[:, None])
    place = offset * CAP + jnp.sum(earlier, axis=1, dtype=jnp.int32)
    chosen = place[None, :] == jnp.arange(n_row * CAP, dtype=jnp.int32)[:, None]

    def pick(values):
        return jnp.sum(jnp.where(chosen, values[None, :], 0), axis=1, dtype=jnp.int32)

    used = jnp.any(chosen, axis=1)
    return pick(order), pick(slot), jnp.where(used, pick(target), row_count)


def local(
    nodes, weight, adjacency, history, pull_owner, pull_slot, pull_target, hist_tiles, cotangent
):
    n_row, n_col = lax.axis_size("row"), lax.axis_size("col")
    span, hid = nodes.shape
    panel, columns = adjacency.shape
    row_count = panel // BLK
    chips = list(range(2, n_row, 2))

    near = {0: nodes, **{t: swap(nodes, "row", t) for t in chips}}
    near.update({t ^ 1: swap(x, "row", 1) for t, x in list(near.items())})

    middle = history.shape[0] // 2
    bits = [1 << b for b in range(1, n_row.bit_length() - 1)]
    halves = []
    for half, order in ((history[:middle], bits), (history[middle:], bits[::-1])):
        held = {0: half}
        for bit in order:
            held.update({t ^ bit: swap(x, "row", bit) for t, x in list(held.items())})
        held.update({t ^ 1: swap(x, "row", 1) for t, x in list(held.items())})
        halves += [held[t] for t in range(n_row)]

    parts = call(
        functools.partial(aggregate_kernel, n_row, n_col),
        [shape(span, hid, dtype=BF16 if s else F32) for s in range(n_col)],
        [shape(columns, hid)],
        2 * panel * columns * hid,
        adjacency,
        *[near[t] for t in range(n_row)],
    )
    mixing = parts[0]
    for s in range(1, n_col):
        mixing = mixing + swap(parts[s], "col", s).astype(F32)
    in_batch = jnp.dot(mixing, weight.astype(F32), precision=lax.Precision.HIGHEST)

    lists = pull_lists(pull_owner[:, 0], pull_slot, pull_target, n_row, row_count)
    terms = call(
        functools.partial(history_kernel, n_row, n_col),
        [shape(span, hid, dtype=BF16 if s else F32) for s in range(n_col)],
        [shape(panel + BLK, hid, dtype=F32)],
        2 * n_row * CAP * BLK * BLK * hid,
        *lists,
        hist_tiles,
        *halves,
        specs=[SCALARS] * 3 + [WHOLE] * (1 + 2 * n_row),
    )
    mixed = in_batch + terms[0]
    for s in range(1, n_col):
        mixed = mixed + swap(terms[s], "col", s).astype(F32)

    activated = jax.nn.silu(mixed).astype(BF16)
    sigmoid_z = jax.nn.sigmoid(mixed)
    grad_pre = cotangent.astype(F32) * sigmoid_z * (1.0 + mixed * (1.0 - sigmoid_z))
    flipped = grad_pre.T.astype(BF16)
    pieces = [flipped] + [swap(flipped, "col", s) for s in range(1, n_col)]

    partial_grad = lax.dot_general(
        mixing.astype(BF16), flipped, (((0,), (1,)), ((), ())), preferred_element_type=F32
    )
    mine = lax.axis_index("row") % 2
    split = partial_grad.reshape(2, hid // 2, hid)
    kept = lax.dynamic_index_in_dim(split, mine, 0, keepdims=False)
    given = lax.dynamic_index_in_dim(split, 1 - mine, 0, keepdims=False).astype(BF16)
    kept = kept + swap(given, "row", 1).astype(F32)
    kept = spread_sum(kept, "row", [0] + chips)
    kept = spread_sum(kept, "col", range(n_col))
    kept = kept * (1.0 / math.sqrt(span * n_row * n_col))
    other = swap(kept, "row", 1)
    grad_weight = jnp.where(
        mine == 0,
        jnp.concatenate([kept, other], axis=0),
        jnp.concatenate([other, kept], axis=0),
    )

    flops = panel * columns * hid
    given = call(
        functools.partial(transposed_kernel, n_col, [t ^ 1 for t in chips] + [1]),
        [shape(hid, span)] * (n_row // 2),
        [shape(hid, panel)],
        flops,
        adjacency,
        *pieces,
    )
    kept = call(
        functools.partial(transposed_kernel, n_col, chips + [0]),
        [shape(hid, span, dtype=F32)] * (n_row // 2),
        [shape(hid, panel)],
        flops,
        adjacency,
        *pieces,
    )
    sums = [k + swap(g, "row", 1).astype(F32) for k, g in zip(kept, given, strict=True)]
    total = sums[-1]
    for t, part in zip(chips, sums[:-1], strict=True):
        total = total + swap(part.astype(BF16), "row", t).astype(F32)
    grad_proj = total.astype(BF16)
    grad_nodes = lax.dot_general(
        grad_proj, weight, (((0,), (1,)), ((), ())), preferred_element_type=F32
    ).astype(BF16)
    return (activated, grad_nodes, grad_weight)


def solution(mesh):
    return jax.shard_map(
        local,
        mesh=mesh,
        in_specs=(
            P(("row", "col"), None),
            P(),
            P("row", "col"),
            P(("row", "col"), None),
            P(("row", "col"), None),
            P(("row", "col")),
            P(("row", "col")),
            P(("row", "col"), None, None),
            P(("row", "col"), None),
        ),
        out_specs=(P(("row", "col"), None), P(("row", "col"), None), P()),
        check_vma=False,
    )
```

```python
import functools
import math

import jax
import jax.numpy as jnp
from jax import lax
from jax.experimental import pallas as pl
from jax.experimental.pallas import tpu as pltpu
from jax.sharding import PartitionSpec as P

BLK = 128
CAP = 4
BF16 = jnp.bfloat16
F32 = jnp.float32
WHOLE = pl.BlockSpec(memory_space=pltpu.VMEM)
SCALARS = pl.BlockSpec(memory_space=pltpu.SMEM)


def swap(x, axis, offset):
    size = lax.axis_size(axis)
    return lax.ppermute(x, axis, [(i, i ^ offset) for i in range(size)])


def shape(*dims, dtype=BF16):
    return jax.ShapeDtypeStruct(dims, dtype)


def nbytes(arrays):
    return sum(math.prod(a.shape) * jnp.dtype(a.dtype).itemsize for a in arrays)


def call(kernel, outs, operands, scratch=(), lists=()):
    held = nbytes(outs) + nbytes(scratch)
    operands = [pltpu.with_memory_space_constraint(x, pltpu.VMEM) for x in operands]
    return pl.pallas_call(
        kernel,
        out_shape=outs,
        in_specs=[SCALARS] * len(lists) + [WHOLE] * len(operands),
        out_specs=[WHOLE] * len(outs),
        scratch_shapes=[pltpu.VMEM(x.shape, x.dtype) for x in scratch],
        compiler_params=pltpu.CompilerParams(vmem_limit_bytes=held + (4 << 20)),
        cost_estimate=pl.CostEstimate(flops=0, bytes_accessed=0, transcendentals=0),
    )(*lists, *operands)


def part(index, size):
    return pl.ds(pl.multiple_of(index * size, size), size)


def later_kernel(x_ref, _, out):
    out[...] = x_ref[...]


def add_kernel(x_ref, y_ref, _, out):
    out[...] = (x_ref[...].astype(F32) + y_ref[...].astype(F32)).astype(out.dtype)


def stack_kernel(*refs):
    for i, ref in enumerate(refs[:-2]):
        refs[-1][i] = ref[...]


def lists_kernel(held, spare, owner, slot, target, _, which, code, which2, code2, count):
    r = lax.axis_index("row")
    for refs in ((which, code), (which2, code2)):
        for i in range(refs[0].shape[0]):
            refs[0][i] = 0
            refs[1][i] = spare * held
    for t in range(count.shape[0]):
        count[t] = 0

    def place(k, _):
        t = owner[0, k] ^ r
        i = t // 2 * CAP + count[t]
        count[t] += 1

        @pl.when(t % 2 == 0)
        def _():
            which[i] = k
            code[i] = target[k] * held + slot[k]

        @pl.when(t % 2 == 1)
        def _():
            which2[i] = k
            code2[i] = target[k] * held + slot[k]

        return 0

    lax.fori_loop(0, slot.shape[0], place, 0)


def tiles_kernel(which, tiles, out):
    for i in range(out.shape[0]):
        out[i] = tiles[which[i]]


def aggregate_kernel(n_row, n_col, _, a_ref, own, other, near, across, __, keep, send, x_ref):
    span = own.shape[0]
    r, c = lax.axis_index("row"), lax.axis_index("col")
    x_ref[part(r, span), :] = own[...]
    x_ref[part(r ^ 1, span), :] = other[...]
    for t in range(2, n_row):
        x_ref[part(r ^ t, span), :] = (across if t % 2 else near)[t // 2 - 1]
    for s in range(n_col):
        block = jnp.dot(a_ref[part(c ^ s, span), :], x_ref[...], preferred_element_type=F32)
        if s % 2:
            send[s // 2] = block.astype(BF16)
        else:
            keep[s // 2] = block


def halve_kernel(kept, received, keep, send):
    for i in range(kept.shape[0]):
        block = kept[i] + received[i].astype(F32)
        if i % 2:
            send[i // 2] = block.astype(BF16)
        else:
            keep[i // 2] = block


def project_kernel(kept, received, w_ref, projected, flipped):
    total = kept[0] + received[0].astype(F32)
    high = total.astype(BF16)
    low = (total - high.astype(F32)).astype(BF16)
    projected[...] = jnp.dot(high, w_ref[...], preferred_element_type=F32) + jnp.dot(
        low, w_ref[...], preferred_element_type=F32
    )
    flipped[...] = total.T.astype(BF16)


def add_pulls(pulls, held, code, tile_of, acc):
    for i, piece in pulls:
        block = piece[part(code[i] % held, BLK), :]
        rows = part(code[i] // held, BLK)
        acc[rows, :] += jnp.dot(tile_of(i), block, preferred_element_type=F32)


def pulls_of(chips, pieces):
    return [
        (i * CAP + m, piece)
        for i, piece in zip(chips, pieces, strict=True)
        for m in range(CAP)
    ]


def early_kernel(offsets, held, which, code, code2, projected, tiles, tiles2, *refs):
    pieces, (own, others) = refs[:-2], refs[-2:]
    pulls = pulls_of(offsets, pieces)
    span = projected.shape[0]
    own[...] = jnp.zeros_like(own)
    others[...] = jnp.zeros_like(others)
    own[part(lax.axis_index("col"), span), :] = projected[...]
    add_pulls(pulls, held, code2, lambda i: tiles2[i], others)
    add_pulls(pulls, held, code, lambda i: tiles[which[i]], own)


def others_kernel(offsets, held, code, acc_in, tiles, *refs):
    pieces, (out, acc) = refs[:-2], refs[-2:]
    acc[...] = acc_in[...]
    add_pulls(pulls_of(offsets, pieces), held, code, lambda i: tiles[i], acc)
    out[...] = acc[: out.shape[0], :].astype(BF16)


def own_kernel(offsets, held, which, code, acc_in, tiles, *refs):
    pieces, out = refs[:-1], refs[-1]
    out[...] = acc_in[...]
    add_pulls(pulls_of(offsets, pieces), held, code, lambda i: tiles[which[i]], out)


def merge_kernel(n_col, own, received, keep, *sends):
    span = keep.shape[0]
    c = lax.axis_index("col")
    for s in range(n_col):
        rows = part(c ^ s, span)
        block = own[rows, :] + received[rows, :].astype(F32)
        if s:
            sends[s - 1][...] = block.astype(BF16)
        else:
            keep[...] = block


def activate_kernel(cotangent, kept, *refs):
    parts, (activated, flipped) = refs[:-2], refs[-2:]
    mixed = kept[...]
    for ref in parts:
        mixed = mixed + ref[...].astype(F32)
    sigmoid_z = jax.nn.sigmoid(mixed)
    activated[...] = (mixed * sigmoid_z).astype(BF16)
    grad_pre = cotangent[...].astype(F32) * sigmoid_z * (1.0 + mixed * (1.0 - sigmoid_z))
    flipped[...] = grad_pre.T.astype(BF16)


def weight_kernel(x_ref, g_ref, kept, given):
    half = x_ref.shape[0] // 2
    mine = lax.axis_index("row") % 2
    for out, core in ((kept, mine), (given, 1 - mine)):
        product = lax.dot_general(
            x_ref[part(core, half), :],
            g_ref[...],
            (((1,), (1,)), ((), ())),
            preferred_element_type=F32,
        )
        out[...] = product.astype(out.dtype)


def join_kernel(kept, received, flipped, total, joined):
    total[...] = (kept[...] + received[...].astype(F32)).astype(BF16)
    joined[: flipped.shape[0], :] = flipped[...]
    joined[flipped.shape[0] :, :] = total[...]


def joined_kernel(at, kept, received, out):
    out[...] = (kept[...].astype(F32) + received[at:, :].astype(F32)).astype(BF16)


def panel_kernel(*refs):
    pieces, out = refs[:-1], refs[-1]
    span = pieces[0].shape[1]
    c = lax.axis_index("col")
    for s, piece in enumerate(pieces):
        out[:, part(c ^ s, span)] = piece[: out.shape[0], :]


def transposed_kernel(offsets, a_ref, g_ref, _, given, kept):
    span = kept.shape[2]
    r = lax.axis_index("row")
    for out, core in ((given, 1), (kept, 0)):
        for i, t in enumerate(offsets):
            columns = part(r ^ t ^ core, span)
            product = jnp.dot(g_ref[...], a_ref[:, columns], preferred_element_type=F32)
            out[i] = product.astype(out.dtype)


def tree_kernel(*refs):
    terms, out = [ref[...].astype(F32) for ref in refs[:-2]], refs[-1]
    while len(terms) > 1:
        terms = [a + b for a, b in zip(terms[::2], terms[1::2], strict=True)]
    out[...] = terms[0].astype(out.dtype)


def cores_kernel(kept, received, own, *sends):
    own[...] = kept[0] + received[0].astype(F32)
    for i, send in enumerate(sends, 1):
        send[...] = (kept[i] + received[i].astype(F32)).astype(BF16)


def reduce_columns(keep, send, span, hid):
    bit = 1
    while True:
        received = swap(send, "col", bit)
        count = keep.shape[0]
        if count == 1:
            return keep, received
        bit *= 2
        keep, send = call(
            halve_kernel,
            [shape(count // 2, span, hid, dtype=F32), shape(count // 2, span, hid)],
            [keep, received],
        )


def local(
    nodes, weight, adjacency, history, pull_owner, pull_slot, pull_target, hist_tiles, cotangent
):
    n_row, n_col = lax.axis_size("row"), lax.axis_size("col")
    span, hid = nodes.shape
    panel, columns = adjacency.shape
    row_count = panel // BLK
    chips = list(range(0, n_row, 2))

    beside = swap(nodes, "row", 1)
    near = [swap(nodes, "row", t) for t in chips[:0:-1]][::-1]
    (history,) = call(later_kernel, [shape(*history.shape)], [history, beside])
    (stacked,) = call(stack_kernel, [shape(len(near), span, hid)], [*near, history])
    across = swap(stacked, "row", 1)

    blocks_held = history.shape[0] // BLK
    places = len(chips) * CAP
    which, code, which2, code2 = pl.pallas_call(
        functools.partial(lists_kernel, blocks_held, row_count),
        out_shape=[shape(places, dtype=jnp.int32)] * 4,
        in_specs=[SCALARS] * 3 + [WHOLE],
        out_specs=[SCALARS] * 4,
        scratch_shapes=[pltpu.SMEM((n_row,), jnp.int32)],
        compiler_params=pltpu.CompilerParams(vmem_limit_bytes=4 << 20),
    )(pull_owner.T, pull_slot, pull_target, history)
    (tiles,) = call(tiles_kernel, [shape(places, BLK, BLK)], [hist_tiles], lists=[which2])
    tiles = swap(tiles, "row", 1)
    code2 = swap(code2, "row", 1)

    blocks = [shape(n_col // 2, span, hid, dtype=F32), shape(n_col // 2, span, hid)]
    keep, send = call(
        functools.partial(aggregate_kernel, n_row, n_col),
        blocks,
        [adjacency, nodes, beside, stacked, across, tiles],
        [shape(columns, hid)],
        [code2],
    )
    keep, received = reduce_columns(keep, send, span, hid)
    projected, summed = call(
        project_kernel, [shape(span, hid, dtype=F32), shape(hid, span)], [keep, received, weight]
    )

    past = [history] + [swap(history, "row", t) for t in chips[1:]]
    early = [i for i, t in enumerate(chips) if t & (t - 1) == 0]
    late = [i for i, t in enumerate(chips) if t & (t - 1)]

    spare = shape(panel + BLK, hid, dtype=F32)
    own_terms, terms = call(
        functools.partial(early_kernel, early, blocks_held),
        [spare, spare],
        [projected, hist_tiles, tiles, *[past[i] for i in early]],
        lists=[which, code, code2],
    )
    (given,) = call(
        functools.partial(others_kernel, late, blocks_held),
        [shape(panel, hid)],
        [terms, tiles, *[past[i] for i in late]],
        [spare],
        [code2],
    )
    received = swap(given, "row", 1)
    (terms,) = call(
        functools.partial(own_kernel, late, blocks_held),
        [spare],
        [own_terms, hist_tiles, *[past[i] for i in late]],
        lists=[which, code],
    )
    keep, *sends = call(
        functools.partial(merge_kernel, n_col),
        [shape(span, hid, dtype=BF16 if s else F32) for s in range(n_col)],
        [terms, received],
    )
    activated, flipped = call(
        activate_kernel,
        [shape(span, hid), shape(hid, span)],
        [cotangent, keep, *[swap(send, "col", s) for s, send in enumerate(sends, 1)]],
    )

    kept, given = call(
        weight_kernel,
        [shape(hid // 2, hid, dtype=F32), shape(hid // 2, hid)],
        [summed, flipped],
    )
    kept, joined = call(
        join_kernel,
        [shape(hid // 2, hid), shape(hid + hid // 2, span)],
        [kept, swap(given, "row", 1), flipped],
    )
    pieces = [flipped, swap(joined, "col", 1)]
    pieces += [swap(flipped, "col", s) for s in range(2, n_col)]
    (kept,) = call(
        functools.partial(joined_kernel, hid), [shape(hid // 2, hid)], [kept, pieces[1]]
    )
    gradients = call(panel_kernel, [shape(hid, panel)], pieces)[0]
    (halfway,) = call(
        tree_kernel,
        [shape(hid // 2, hid)],
        [*[swap(kept, "row", t) if t else kept for t in chips], gradients],
    )

    given, kept = call(
        functools.partial(transposed_kernel, chips),
        [shape(len(chips), hid, span, dtype=dtype) for dtype in (BF16, F32)],
        [adjacency, gradients, halfway],
    )
    received = swap(given, "row", 1)
    total, *sends = call(
        cores_kernel,
        [shape(hid, span, dtype=BF16 if t else F32) for t in chips],
        [kept, received],
    )
    arrived = [swap(send, "row", t) for t, send in zip(chips[1:], sends, strict=True)]
    for x in arrived:
        total = total + x.astype(F32)
    grad_proj = total.astype(BF16)
    grad_nodes = lax.dot_general(
        grad_proj, weight, (((0,), (1,)), ((), ())), preferred_element_type=F32
    ).astype(BF16)

    for bit in [1 << b for b in range(1, n_col.bit_length() - 1)]:
        received = swap(halfway, "col", bit)
        (halfway,) = call(add_kernel, [shape(*halfway.shape)], [halfway, received, arrived[0]])
    other = swap(halfway, "row", 1)
    even = lax.axis_index("row") % 2 == 0
    grad_weight = jnp.concatenate(
        [jnp.where(even, halfway, other), jnp.where(even, other, halfway)], axis=0
    ).astype(F32) * (1.0 / math.sqrt(span * n_row * n_col))
    return (activated, grad_nodes, grad_weight)


def solution(mesh):
    return jax.shard_map(
        local,
        mesh=mesh,
        in_specs=(
            P(("row", "col"), None),
            P(),
            P("row", "col"),
            P(("row", "col"), None),
            P(("row", "col"), None),
            P(("row", "col")),
            P(("row", "col")),
            P(("row", "col"), None, None),
            P(("row", "col"), None),
        ),
        out_specs=(P(("row", "col"), None), P(("row", "col"), None), P()),
        check_vma=False,
    )
```

```python
import functools
import math

import jax
import jax.numpy as jnp
from jax import lax
from jax.experimental import pallas as pl
from jax.experimental.pallas import tpu as pltpu
from jax.sharding import PartitionSpec as P

BLK = 128
CAP = 4
BF16 = jnp.bfloat16
F32 = jnp.float32
WHOLE = pl.BlockSpec(memory_space=pltpu.VMEM)
SCALARS = pl.BlockSpec(memory_space=pltpu.SMEM)


def swap(x, axis, offset):
    size = lax.axis_size(axis)
    return lax.ppermute(x, axis, [(i, i ^ offset) for i in range(size)])


def shape(*dims, dtype=BF16):
    return jax.ShapeDtypeStruct(dims, dtype)


def nbytes(arrays):
    return sum(math.prod(a.shape) * jnp.dtype(a.dtype).itemsize for a in arrays)


def call(kernel, outs, operands, scratch=(), lists=()):
    held = nbytes(outs) + nbytes(scratch)
    operands = [pltpu.with_memory_space_constraint(x, pltpu.VMEM) for x in operands]
    return pl.pallas_call(
        kernel,
        out_shape=outs,
        in_specs=[SCALARS] * len(lists) + [WHOLE] * len(operands),
        out_specs=[WHOLE] * len(outs),
        scratch_shapes=[pltpu.VMEM(x.shape, x.dtype) for x in scratch],
        compiler_params=pltpu.CompilerParams(vmem_limit_bytes=held + (4 << 20)),
        cost_estimate=pl.CostEstimate(flops=0, bytes_accessed=0, transcendentals=0),
    )(*lists, *operands)


def part(index, size):
    return pl.ds(pl.multiple_of(index * size, size), size)


def later_kernel(x_ref, _, out):
    out[...] = x_ref[...]


def add_kernel(x_ref, y_ref, _, out):
    out[...] = (x_ref[...].astype(F32) + y_ref[...].astype(F32)).astype(out.dtype)


def stack_kernel(*refs):
    for i, ref in enumerate(refs[:-2]):
        refs[-1][i] = ref[...]


def lists_kernel(held, spare, owner, slot, target, _, which, code, which2, code2, count):
    r = lax.axis_index("row")
    for refs in ((which, code), (which2, code2)):
        for i in range(refs[0].shape[0]):
            refs[0][i] = 0
            refs[1][i] = spare * held
    for t in range(count.shape[0]):
        count[t] = 0

    def place(k, _):
        t = owner[0, k] ^ r
        i = t // 2 * CAP + count[t]
        count[t] += 1

        @pl.when(t % 2 == 0)
        def _():
            which[i] = k
            code[i] = target[k] * held + slot[k]

        @pl.when(t % 2 == 1)
        def _():
            which2[i] = k
            code2[i] = target[k] * held + slot[k]

        return 0

    lax.fori_loop(0, slot.shape[0], place, 0)


def tiles_kernel(which, tiles, out):
    for i in range(out.shape[0]):
        out[i] = tiles[which[i]]


def aggregate_kernel(n_row, n_col, _, a_ref, own, other, near, across, __, keep, send, x_ref):
    span = own.shape[0]
    r, c = lax.axis_index("row"), lax.axis_index("col")
    x_ref[part(r, span), :] = own[...]
    x_ref[part(r ^ 1, span), :] = other[...]
    for t in range(2, n_row):
        x_ref[part(r ^ t, span), :] = (across if t % 2 else near)[t // 2 - 1]
    for s in range(n_col):
        block = jnp.dot(a_ref[part(c ^ s, span), :], x_ref[...], preferred_element_type=F32)
        if s % 2:
            send[s // 2] = block.astype(BF16)
        else:
            keep[s // 2] = block


def halve_kernel(kept, received, keep, send):
    for i in range(kept.shape[0]):
        block = kept[i] + received[i].astype(F32)
        if i % 2:
            send[i // 2] = block.astype(BF16)
        else:
            keep[i // 2] = block


def project_kernel(kept, received, w_ref, projected, flipped):
    total = kept[0] + received[0].astype(F32)
    high = total.astype(BF16)
    low = (total - high.astype(F32)).astype(BF16)
    projected[...] = jnp.dot(high, w_ref[...], preferred_element_type=F32) + jnp.dot(
        low, w_ref[...], preferred_element_type=F32
    )
    flipped[...] = total.T.astype(BF16)


def add_pulls(pulls, held, code, tile_of, acc):
    for i, piece in pulls:
        block = piece[part(code[i] % held, BLK), :]
        rows = part(code[i] // held, BLK)
        acc[rows, :] += jnp.dot(tile_of(i), block, preferred_element_type=F32)


def pulls_of(chips, pieces):
    return [
        (i * CAP + m, piece)
        for i, piece in zip(chips, pieces, strict=True)
        for m in range(CAP)
    ]


def early_kernel(offsets, held, which, code, code2, projected, tiles, tiles2, *refs):
    pieces, (own, others) = refs[:-2], refs[-2:]
    pulls = pulls_of(offsets, pieces)
    span = projected.shape[0]
    own[...] = jnp.zeros_like(own)
    others[...] = jnp.zeros_like(others)
    own[part(lax.axis_index("col"), span), :] = projected[...]
    add_pulls(pulls, held, code2, lambda i: tiles2[i], others)
    add_pulls(pulls, held, code, lambda i: tiles[which[i]], own)


def others_kernel(offsets, held, code, acc_in, tiles, *refs):
    pieces, (out, acc) = refs[:-2], refs[-2:]
    acc[...] = acc_in[...]
    add_pulls(pulls_of(offsets, pieces), held, code, lambda i: tiles[i], acc)
    out[...] = acc[: out.shape[0], :].astype(BF16)


def own_kernel(offsets, held, which, code, acc_in, tiles, *refs):
    pieces, out = refs[:-1], refs[-1]
    out[...] = acc_in[...]
    add_pulls(pulls_of(offsets, pieces), held, code, lambda i: tiles[which[i]], out)


def merge_kernel(n_col, own, received, keep, *sends):
    span = keep.shape[0]
    c = lax.axis_index("col")
    for s in range(n_col):
        rows = part(c ^ s, span)
        block = own[rows, :] + received[rows, :].astype(F32)
        if s:
            sends[s - 1][...] = block.astype(BF16)
        else:
            keep[...] = block


def activate_kernel(cotangent, kept, *refs):
    parts, (activated, flipped) = refs[:-2], refs[-2:]
    mixed = kept[...]
    for ref in parts:
        mixed = mixed + ref[...].astype(F32)
    sigmoid_z = jax.nn.sigmoid(mixed)
    activated[...] = (mixed * sigmoid_z).astype(BF16)
    grad_pre = cotangent[...].astype(F32) * sigmoid_z * (1.0 + mixed * (1.0 - sigmoid_z))
    flipped[...] = grad_pre.T.astype(BF16)


def weight_kernel(x_ref, g_ref, kept, given):
    half = x_ref.shape[0] // 2
    mine = lax.axis_index("row") % 2
    for out, core in ((kept, mine), (given, 1 - mine)):
        product = lax.dot_general(
            x_ref[part(core, half), :],
            g_ref[...],
            (((1,), (1,)), ((), ())),
            preferred_element_type=F32,
        )
        out[...] = product.astype(out.dtype)


def panel_kernel(*refs):
    pieces, out = refs[:-1], refs[-1]
    span = pieces[0].shape[1]
    c = lax.axis_index("col")
    for s, piece in enumerate(pieces):
        out[:, part(c ^ s, span)] = piece[: out.shape[0], :]


def transposed_kernel(offsets, a_ref, g_ref, _, given, kept):
    span = kept.shape[2]
    r = lax.axis_index("row")
    for out, core in ((given, 1), (kept, 0)):
        for i, t in enumerate(offsets):
            columns = part(r ^ t ^ core, span)
            product = jnp.dot(g_ref[...], a_ref[:, columns], preferred_element_type=F32)
            out[i] = product.astype(out.dtype)


def tree_kernel(*refs):
    terms, out = [ref[...].astype(F32) for ref in refs[:-2]], refs[-1]
    while len(terms) > 1:
        terms = [a + b for a, b in zip(terms[::2], terms[1::2], strict=True)]
    out[...] = terms[0].astype(out.dtype)


def cores_kernel(places, kept, received, _, *outs):
    for i, out in zip(places, outs, strict=True):
        out[...] = (kept[i] + received[i].astype(F32)).astype(out.dtype)


def reduce_columns(keep, send, span, hid):
    bit = 1
    while True:
        received = swap(send, "col", bit)
        count = keep.shape[0]
        if count == 1:
            return keep, received
        bit *= 2
        keep, send = call(
            halve_kernel,
            [shape(count // 2, span, hid, dtype=F32), shape(count // 2, span, hid)],
            [keep, received],
        )


def local(
    nodes, weight, adjacency, history, pull_owner, pull_slot, pull_target, hist_tiles, cotangent
):
    n_row, n_col = lax.axis_size("row"), lax.axis_size("col")
    span, hid = nodes.shape
    panel, columns = adjacency.shape
    row_count = panel // BLK
    chips = list(range(0, n_row, 2))

    beside = swap(nodes, "row", 1)
    near = [swap(nodes, "row", t) for t in chips[:0:-1]][::-1]
    (history,) = call(later_kernel, [shape(*history.shape)], [history, beside])
    (stacked,) = call(stack_kernel, [shape(len(near), span, hid)], [*near, history])
    across = swap(stacked, "row", 1)

    blocks_held = history.shape[0] // BLK
    places = len(chips) * CAP
    which, code, which2, code2 = pl.pallas_call(
        functools.partial(lists_kernel, blocks_held, row_count),
        out_shape=[shape(places, dtype=jnp.int32)] * 4,
        in_specs=[SCALARS] * 3 + [WHOLE],
        out_specs=[SCALARS] * 4,
        scratch_shapes=[pltpu.SMEM((n_row,), jnp.int32)],
        compiler_params=pltpu.CompilerParams(vmem_limit_bytes=4 << 20),
    )(pull_owner.T, pull_slot, pull_target, history)
    (tiles,) = call(tiles_kernel, [shape(places, BLK, BLK)], [hist_tiles], lists=[which2])
    tiles = swap(tiles, "row", 1)
    code2 = swap(code2, "row", 1)

    blocks = [shape(n_col // 2, span, hid, dtype=F32), shape(n_col // 2, span, hid)]
    keep, send = call(
        functools.partial(aggregate_kernel, n_row, n_col),
        blocks,
        [adjacency, nodes, beside, stacked, across, tiles],
        [shape(columns, hid)],
        [code2],
    )
    keep, received = reduce_columns(keep, send, span, hid)
    projected, summed = call(
        project_kernel, [shape(span, hid, dtype=F32), shape(hid, span)], [keep, received, weight]
    )

    past = [history] + [swap(history, "row", t) for t in chips[1:]]
    early = [i for i, t in enumerate(chips) if t & (t - 1) == 0]
    late = [i for i, t in enumerate(chips) if t & (t - 1)]

    spare = shape(panel + BLK, hid, dtype=F32)
    own_terms, terms = call(
        functools.partial(early_kernel, early, blocks_held),
        [spare, spare],
        [projected, hist_tiles, tiles, *[past[i] for i in early]],
        lists=[which, code, code2],
    )
    (given,) = call(
        functools.partial(others_kernel, late, blocks_held),
        [shape(panel, hid)],
        [terms, tiles, *[past[i] for i in late]],
        [spare],
        [code2],
    )
    received = swap(given, "row", 1)
    (terms,) = call(
        functools.partial(own_kernel, late, blocks_held),
        [spare],
        [own_terms, hist_tiles, *[past[i] for i in late]],
        lists=[which, code],
    )
    keep, *sends = call(
        functools.partial(merge_kernel, n_col),
        [shape(span, hid, dtype=BF16 if s else F32) for s in range(n_col)],
        [terms, received],
    )
    activated, flipped = call(
        activate_kernel,
        [shape(span, hid), shape(hid, span)],
        [cotangent, keep, *[swap(send, "col", s) for s, send in enumerate(sends, 1)]],
    )

    pieces = [swap(flipped, "col", s) if s else flipped for s in range(n_col)]
    kept, given = call(
        weight_kernel,
        [shape(hid // 2, hid, dtype=F32), shape(hid // 2, hid)],
        [summed, flipped],
    )
    kept = (kept + swap(given, "row", 1).astype(F32)).astype(BF16)
    gradients = call(panel_kernel, [shape(hid, panel)], pieces)[0]
    (halfway,) = call(
        tree_kernel,
        [shape(hid // 2, hid)],
        [*[swap(kept, "row", t) if t else kept for t in chips], gradients],
    )

    given, kept = call(
        functools.partial(transposed_kernel, chips),
        [shape(len(chips), hid, span, dtype=dtype) for dtype in (BF16, F32)],
        [adjacency, gradients, halfway],
    )
    received = swap(given, "row", 1)
    arrived, token = {}, given
    for places in (list(range(2, len(chips))), [0, 1]):
        sums = call(
            functools.partial(cores_kernel, places),
            [shape(hid, span, dtype=BF16 if i else F32) for i in places],
            [kept, received, token],
        )
        for i, x in zip(places, sums, strict=True):
            arrived[i] = swap(x, "row", chips[i]) if i else x
        if token is given:
            beside = swap(halfway, "col", 1)
            (token,) = call(add_kernel, [shape(*halfway.shape)], [halfway, beside, sums[0]])
    halfway = token
    total = arrived[0]
    for i in range(1, len(chips)):
        total = total + arrived[i].astype(F32)
    grad_proj = total.astype(BF16)
    grad_nodes = lax.dot_general(
        grad_proj, weight, (((0,), (1,)), ((), ())), preferred_element_type=F32
    ).astype(BF16)

    for bit in [1 << b for b in range(1, n_col.bit_length() - 1)]:
        received = swap(halfway, "col", bit)
        (halfway,) = call(add_kernel, [shape(*halfway.shape)], [halfway, received, arrived[len(chips) - 1]])
    other = swap(halfway, "row", 1)
    even = lax.axis_index("row") % 2 == 0
    grad_weight = jnp.concatenate(
        [jnp.where(even, halfway, other), jnp.where(even, other, halfway)], axis=0
    ).astype(F32) * (1.0 / math.sqrt(span * n_row * n_col))
    return (activated, grad_nodes, grad_weight)


def solution(mesh):
    return jax.shard_map(
        local,
        mesh=mesh,
        in_specs=(
            P(("row", "col"), None),
            P(),
            P("row", "col"),
            P(("row", "col"), None),
            P(("row", "col"), None),
            P(("row", "col")),
            P(("row", "col")),
            P(("row", "col"), None, None),
            P(("row", "col"), None),
        ),
        out_specs=(P(("row", "col"), None), P(("row", "col"), None), P()),
        check_vma=False,
    )
```

```python
import functools
import math

import jax
import jax.numpy as jnp
from jax import lax
from jax.experimental import pallas as pl
from jax.experimental.pallas import tpu as pltpu
from jax.sharding import PartitionSpec as P

BLK = 128
CAP = 4
BF16 = jnp.bfloat16
F32 = jnp.float32
WHOLE = pl.BlockSpec(memory_space=pltpu.VMEM)
SCALARS = pl.BlockSpec(memory_space=pltpu.SMEM)


def swap(x, axis, offset):
    size = lax.axis_size(axis)
    return lax.ppermute(x, axis, [(i, i ^ offset) for i in range(size)])


def shape(*dims, dtype=BF16):
    return jax.ShapeDtypeStruct(dims, dtype)


def column_offsets(n_col):
    return [n_col - 1, *range(1, n_col - 1)]


def nbytes(arrays):
    return sum(math.prod(a.shape) * jnp.dtype(a.dtype).itemsize for a in arrays)


def call(kernel, outs, operands, scratch=(), lists=()):
    held = nbytes(outs) + nbytes(scratch)
    operands = [pltpu.with_memory_space_constraint(x, pltpu.VMEM) for x in operands]
    return pl.pallas_call(
        kernel,
        out_shape=outs,
        in_specs=[SCALARS] * len(lists) + [WHOLE] * len(operands),
        out_specs=[WHOLE] * len(outs),
        scratch_shapes=[pltpu.VMEM(x.shape, x.dtype) for x in scratch],
        compiler_params=pltpu.CompilerParams(vmem_limit_bytes=held + (4 << 20)),
        cost_estimate=pl.CostEstimate(flops=0, bytes_accessed=0, transcendentals=0),
    )(*lists, *operands)


def part(index, size):
    return pl.ds(pl.multiple_of(index * size, size), size)


def later_kernel(x_ref, _, out):
    out[...] = x_ref[...]


def add_kernel(x_ref, y_ref, _, out):
    out[...] = (x_ref[...].astype(F32) + y_ref[...].astype(F32)).astype(out.dtype)


def stack_kernel(*refs):
    for i, ref in enumerate(refs[:-3]):
        refs[-1][i] = ref[...]


def lists_kernel(held, spare, mine, theirs, _, which, code, which2, code2, count):
    r = lax.axis_index("row")
    for refs in ((which, code), (which2, code2)):
        for i in range(refs[0].shape[0]):
            refs[0][i] = 0
            refs[1][i] = spare * held
    for t in range(count.shape[0]):
        count[t] = 0

    def place(k, _):
        for pulls, refs, at in (
            (mine, (which, code), 0),
            (theirs, (which2, code2), count.shape[0] // 2),
        ):
            t = pulls[0, k] ^ r

            @pl.when(t % 2 == 0)
            def _(pulls=pulls, refs=refs, at=at, t=t):
                chip = t // 2
                i = chip * CAP + count[at + chip]
                count[at + chip] += 1
                refs[0][i] = k
                refs[1][i] = pulls[2, k] * held + pulls[1, k]

        return 0

    lax.fori_loop(0, mine.shape[1], place, 0)


def aggregate_kernel(n_row, n_col, a_ref, own, other, near, across, keep, send, x_ref):
    span = own.shape[0]
    r, c = lax.axis_index("row"), lax.axis_index("col")
    x_ref[part(r, span), :] = own[...]
    x_ref[part(r ^ 1, span), :] = other[...]
    for t in range(2, n_row):
        x_ref[part(r ^ t, span), :] = (across if t % 2 else near)[t // 2 - 1]
    for s in range(n_col):
        block = jnp.dot(a_ref[part(c ^ s, span), :], x_ref[...], preferred_element_type=F32)
        if s % 2:
            send[s // 2] = block.astype(BF16)
        else:
            keep[s // 2] = block


def halve_kernel(kept, received, keep, send):
    for i in range(kept.shape[0]):
        block = kept[i] + received[i].astype(F32)
        if i % 2:
            send[i // 2] = block.astype(BF16)
        else:
            keep[i // 2] = block


def project_kernel(kept, received, w_ref, projected, flipped):
    total = kept[0] + received[0].astype(F32)
    high = total.astype(BF16)
    low = (total - high.astype(F32)).astype(BF16)
    projected[...] = jnp.dot(high, w_ref[...], preferred_element_type=F32) + jnp.dot(
        low, w_ref[...], preferred_element_type=F32
    )
    flipped[...] = total.T.astype(BF16)


def add_pulls(pulls, held, code, tile_of, acc):
    for i, piece in pulls:
        block = piece[part(code[i] % held, BLK), :]
        rows = part(code[i] // held, BLK)
        acc[rows, :] += jnp.dot(tile_of(i), block, preferred_element_type=F32)


def pulls_of(chips, pieces):
    return [
        (i * CAP + m, piece)
        for i, piece in zip(chips, pieces, strict=True)
        for m in range(CAP)
    ]


def early_kernel(offsets, held, which, code, which2, code2, projected, tiles, tiles2, *refs):
    pieces, (own, others) = refs[:-2], refs[-2:]
    pulls = pulls_of(offsets, pieces)
    span = projected.shape[0]
    own[...] = jnp.zeros_like(own)
    others[...] = jnp.zeros_like(others)
    own[part(lax.axis_index("col"), span), :] = projected[...]
    add_pulls(pulls, held, code2, lambda i: tiles2[which2[i]], others)
    add_pulls(pulls, held, code, lambda i: tiles[which[i]], own)


def others_kernel(offsets, held, which, code, acc_in, tiles, *refs):
    pieces, (out, acc) = refs[:-2], refs[-2:]
    acc[...] = acc_in[...]
    add_pulls(pulls_of(offsets, pieces), held, code, lambda i: tiles[which[i]], acc)
    out[...] = acc[: out.shape[0], :].astype(BF16)


def own_kernel(offsets, held, which, code, acc_in, tiles, *refs):
    pieces, out = refs[:-1], refs[-1]
    out[...] = acc_in[...]
    add_pulls(pulls_of(offsets, pieces), held, code, lambda i: tiles[which[i]], out)


def merge_kernel(n_col, own, received, keep, *sends):
    span = keep.shape[0]
    c = lax.axis_index("col")
    for s in range(n_col):
        rows = part(c ^ s, span)
        block = own[rows, :] + received[rows, :].astype(F32)
        if s:
            sends[s - 1][...] = block.astype(BF16)
        else:
            keep[...] = block


def gradient_kernel(cotangent, kept, *refs):
    parts, (mixed_out, flipped) = refs[:-2], refs[-2:]
    mixed = kept[...]
    for ref in parts:
        mixed = mixed + ref[...].astype(F32)
    mixed_out[...] = mixed
    sigmoid_z = jax.nn.sigmoid(mixed)
    grad_pre = cotangent[...].astype(F32) * sigmoid_z * (1.0 + mixed * (1.0 - sigmoid_z))
    flipped[...] = grad_pre.T.astype(BF16)


def activate_kernel(mixed, kept, received, activated, total):
    activated[...] = (mixed[...] * jax.nn.sigmoid(mixed[...])).astype(BF16)
    total[...] = (kept[...] + received[...].astype(F32)).astype(BF16)


def scale_kernel(scale, mine, other, out):
    half = mine.shape[0]
    core = lax.axis_index("row") % 2
    out[part(core, half), :] = mine[...].astype(F32) * scale
    out[part(1 - core, half), :] = other[...].astype(F32) * scale


def nodes_kernel(w_ref, *refs):
    refs, out = refs[:-1], refs[-1]
    total = refs[0][...]
    for ref in refs[1:]:
        total = total + ref[...].astype(F32)
    out[...] = lax.dot_general(
        total.T.astype(BF16), w_ref[...], (((1,), (1,)), ((), ())), preferred_element_type=F32
    ).astype(BF16)


def weight_kernel(x_ref, g_ref, kept, given):
    half = x_ref.shape[0] // 2
    mine = lax.axis_index("row") % 2
    for out, core in ((kept, mine), (given, 1 - mine)):
        product = lax.dot_general(
            x_ref[part(core, half), :],
            g_ref[...],
            (((1,), (1,)), ((), ())),
            preferred_element_type=F32,
        )
        out[...] = product.astype(out.dtype)


def panel_kernel(offsets, *refs):
    pieces, out = refs[:-1], refs[-1]
    span = pieces[0].shape[1]
    c = lax.axis_index("col")
    for s, piece in zip(offsets, pieces, strict=True):
        out[:, part(c ^ s, span)] = piece[...]


def transposed_kernel(offsets, a_ref, g_ref, _, given, kept):
    span = kept.shape[2]
    r = lax.axis_index("row")
    for out, core in ((given, 1), (kept, 0)):
        for i, t in enumerate(offsets):
            columns = part(r ^ t ^ core, span)
            product = jnp.dot(g_ref[...], a_ref[:, columns], preferred_element_type=F32)
            out[i] = product.astype(out.dtype)


def tree_kernel(*refs):
    terms, out = [ref[...].astype(F32) for ref in refs[:-2]], refs[-1]
    while len(terms) > 1:
        terms = [a + b for a, b in zip(terms[::2], terms[1::2], strict=True)]
    out[...] = terms[0].astype(out.dtype)


def cores_kernel(places, kept, received, _, *outs):
    for i, out in zip(places, outs, strict=True):
        out[...] = (kept[i] + received[i].astype(F32)).astype(out.dtype)


def reduce_columns(keep, send, span, hid):
    bit = 1
    while True:
        received = swap(send, "col", bit)
        count = keep.shape[0]
        if count == 1:
            return keep, received, send
        bit *= 2
        keep, send = call(
            halve_kernel,
            [shape(count // 2, span, hid, dtype=F32), shape(count // 2, span, hid)],
            [keep, received],
        )


def local(
    nodes, weight, adjacency, history, pull_owner, pull_slot, pull_target, hist_tiles, cotangent
):
    n_row, n_col = lax.axis_size("row"), lax.axis_size("col")
    span, hid = nodes.shape
    panel, columns = adjacency.shape
    row_count = panel // BLK
    chips = list(range(0, n_row, 2))
    offsets = column_offsets(n_col)

    pulls = jnp.stack([pull_owner[:, 0], pull_slot, pull_target])
    their_pulls = swap(pulls, "row", 1)
    tiles = swap(hist_tiles, "row", 1)

    beside = swap(nodes, "row", 1)
    near = [swap(nodes, "row", t) for t in chips[:0:-1]][::-1]
    (history,) = call(later_kernel, [shape(*history.shape)], [history, beside])
    (stacked,) = call(stack_kernel, [shape(len(near), span, hid)], [*near, history, tiles])
    across = swap(stacked, "row", 1)

    blocks = [shape(n_col // 2, span, hid, dtype=F32), shape(n_col // 2, span, hid)]
    keep, send = call(
        functools.partial(aggregate_kernel, n_row, n_col),
        blocks,
        [adjacency, nodes, beside, stacked, across],
        [shape(columns, hid)],
    )
    keep, received, halved = reduce_columns(keep, send, span, hid)
    projected, summed = call(
        project_kernel, [shape(span, hid, dtype=F32), shape(hid, span)], [keep, received, weight]
    )

    blocks_held = history.shape[0] // BLK
    places = len(chips) * CAP
    which, code, which2, code2 = pl.pallas_call(
        functools.partial(lists_kernel, blocks_held, row_count),
        out_shape=[shape(places, dtype=jnp.int32)] * 4,
        in_specs=[SCALARS] * 2 + [WHOLE],
        out_specs=[SCALARS] * 4,
        scratch_shapes=[pltpu.SMEM((n_row,), jnp.int32)],
        compiler_params=pltpu.CompilerParams(vmem_limit_bytes=4 << 20),
    )(pulls, their_pulls, halved)

    past = [history] + [swap(history, "row", t) for t in chips[1:]]
    early = [i for i, t in enumerate(chips) if t & (t - 1) == 0]
    late = [i for i, t in enumerate(chips) if t & (t - 1)]

    spare = shape(panel + BLK, hid, dtype=F32)
    own_terms, terms = call(
        functools.partial(early_kernel, early, blocks_held),
        [spare, spare],
        [projected, hist_tiles, tiles, *[past[i] for i in early]],
        lists=[which, code, which2, code2],
    )
    (given,) = call(
        functools.partial(others_kernel, late, blocks_held),
        [shape(panel, hid)],
        [terms, tiles, *[past[i] for i in late]],
        [spare],
        [which2, code2],
    )
    received = swap(given, "row", 1)
    (terms,) = call(
        functools.partial(own_kernel, late, blocks_held),
        [spare],
        [own_terms, hist_tiles, *[past[i] for i in late]],
        lists=[which, code],
    )
    keep, *sends = call(
        functools.partial(merge_kernel, n_col),
        [shape(span, hid, dtype=BF16 if s else F32) for s in range(n_col)],
        [terms, received],
    )
    mixed, flipped = call(
        gradient_kernel,
        [shape(span, hid, dtype=F32), shape(hid, span)],
        [cotangent, keep, *[swap(sends[s - 1], "col", s) for s in offsets]],
    )

    pieces = [swap(flipped, "col", s) if s else flipped for s in [*offsets, 0]]
    kept, given = call(
        weight_kernel,
        [shape(hid // 2, hid, dtype=F32), shape(hid // 2, hid)],
        [summed, flipped],
    )
    activated, kept = call(
        activate_kernel,
        [shape(span, hid), shape(hid // 2, hid)],
        [mixed, kept, swap(given, "row", 1)],
    )
    gradients = call(
        functools.partial(panel_kernel, [*offsets, 0]), [shape(hid, panel)], pieces
    )[0]
    (halfway,) = call(
        tree_kernel,
        [shape(hid // 2, hid)],
        [*[swap(kept, "row", t) if t else kept for t in chips], gradients],
    )

    given, kept = call(
        functools.partial(transposed_kernel, chips),
        [shape(len(chips), hid, span, dtype=dtype) for dtype in (BF16, F32)],
        [adjacency, gradients, halfway],
    )
    received = swap(given, "row", 1)
    arrived, token = {}, given
    for places in (list(range(1, len(chips))), [0]):
        sums = call(
            functools.partial(cores_kernel, places),
            [shape(hid, span, dtype=BF16 if i else F32) for i in places],
            [kept, received, token],
        )
        for i, x in zip(places, sums, strict=True):
            arrived[i] = swap(x, "row", chips[i]) if i else x
        if token is given:
            beside = swap(halfway, "col", 1)
            (token,) = call(add_kernel, [shape(*halfway.shape)], [halfway, beside, sums[0]])
    halfway = token
    (grad_nodes,) = call(
        nodes_kernel, [shape(span, hid)], [weight, *[arrived[i] for i in range(len(chips))]]
    )

    for bit in [1 << b for b in range(1, n_col.bit_length() - 1)]:
        received = swap(halfway, "col", bit)
        (halfway,) = call(add_kernel, [shape(*halfway.shape)], [halfway, received, arrived[len(chips) - 1]])
    scale = 1.0 / math.sqrt(span * n_row * n_col)
    (grad_weight,) = call(
        functools.partial(scale_kernel, scale),
        [shape(hid, hid, dtype=F32)],
        [halfway, swap(halfway, "row", 1)],
    )
    return (activated, grad_nodes, grad_weight)


def solution(mesh):
    return jax.shard_map(
        local,
        mesh=mesh,
        in_specs=(
            P(("row", "col"), None),
            P(),
            P("row", "col"),
            P(("row", "col"), None),
            P(("row", "col"), None),
            P(("row", "col")),
            P(("row", "col")),
            P(("row", "col"), None, None),
            P(("row", "col"), None),
        ),
        out_specs=(P(("row", "col"), None), P(("row", "col"), None), P()),
        check_vma=False,
    )
```

```python
import functools
import math

import jax
import jax.numpy as jnp
from jax import lax
from jax.experimental import pallas as pl
from jax.experimental.pallas import tpu as pltpu
from jax.sharding import PartitionSpec as P

BLK = 128
CAP = 4
BF16 = jnp.bfloat16
F32 = jnp.float32
WHOLE = pl.BlockSpec(memory_space=pltpu.VMEM)
SCALARS = pl.BlockSpec(memory_space=pltpu.SMEM)


def swap(x, axis, offset):
    size = lax.axis_size(axis)
    return lax.ppermute(x, axis, [(i, i ^ offset) for i in range(size)])


def shape(*dims, dtype=BF16):
    return jax.ShapeDtypeStruct(dims, dtype)


def column_offsets(n_col):
    return [n_col - 1, *range(1, n_col - 1)]


def nbytes(arrays):
    return sum(math.prod(a.shape) * jnp.dtype(a.dtype).itemsize for a in arrays)


def call(kernel, outs, operands, scratch=(), lists=()):
    held = nbytes(outs) + nbytes(scratch)
    operands = [pltpu.with_memory_space_constraint(x, pltpu.VMEM) for x in operands]
    return pl.pallas_call(
        kernel,
        out_shape=outs,
        in_specs=[SCALARS] * len(lists) + [WHOLE] * len(operands),
        out_specs=[WHOLE] * len(outs),
        scratch_shapes=[pltpu.VMEM(x.shape, x.dtype) for x in scratch],
        compiler_params=pltpu.CompilerParams(vmem_limit_bytes=held + (4 << 20)),
        cost_estimate=pl.CostEstimate(flops=0, bytes_accessed=0, transcendentals=0),
    )(*lists, *operands)


def part(index, size):
    return pl.ds(pl.multiple_of(index * size, size), size)


def later_kernel(x_ref, *refs):
    out = refs[-1]
    out[...] = x_ref[...]


def add_kernel(x_ref, y_ref, _, *outs):
    rows = outs[0].shape[0]
    for i, out in enumerate(outs):
        at = pl.ds(i * rows, rows)
        out[...] = (x_ref[at, :].astype(F32) + y_ref[at, :].astype(F32)).astype(out.dtype)


def stack_kernel(*refs):
    refs, (_, low, high) = refs[:-3], refs[-3:]
    half = low.shape[1]
    for i, ref in enumerate(refs):
        low[i] = ref[:half, :]
        high[i] = ref[half:, :]


def lists_kernel(held, spare, mine, theirs, _, which, code, which2, code2, count):
    r = lax.axis_index("row")
    for refs in ((which, code), (which2, code2)):
        for i in range(refs[0].shape[0]):
            refs[0][i] = 0
            refs[1][i] = spare * held
    for t in range(count.shape[0]):
        count[t] = 0

    def place(k, _):
        for pulls, refs, at in (
            (mine, (which, code), 0),
            (theirs, (which2, code2), count.shape[0] // 2),
        ):
            t = pulls[0, k] ^ r

            @pl.when(t % 2 == 0)
            def _(pulls=pulls, refs=refs, at=at, t=t):
                chip = t // 2
                i = chip * CAP + count[at + chip]
                count[at + chip] += 1
                refs[0][i] = k
                refs[1][i] = pulls[2, k] * held + pulls[1, k]

        return 0

    lax.fori_loop(0, mine.shape[1], place, 0)


def aggregate_kernel(n_row, n_col, a_ref, own, other, *refs):
    near, (low, high), outs, x_ref = refs[: -3 - n_col], refs[-3 - n_col : -1 - n_col], refs[-1 - n_col : -1], refs[-1]
    span = own.shape[0]
    half = span // 2
    r, c = lax.axis_index("row"), lax.axis_index("col")
    x_ref[part(r, span), :] = own[...]
    x_ref[part(r ^ 1, span), :] = other[...]
    for i, ref in enumerate(near):
        t = 2 * (i + 1)
        x_ref[part(r ^ t, span), :] = ref[...]
        x_ref[part((r ^ t ^ 1) * 2, half), :] = low[i]
        x_ref[part((r ^ t ^ 1) * 2 + 1, half), :] = high[i]
    for s, out in enumerate(outs):
        block = jnp.dot(a_ref[part(c ^ s, span), :], x_ref[...], preferred_element_type=F32)
        out[...] = block.astype(out.dtype)


def halve_kernel(count, *refs):
    kept, received, outs = refs[:count], refs[count : 2 * count], refs[2 * count :]
    for out, x, y in zip(outs, kept, received, strict=True):
        out[...] = (x[...] + y[...].astype(F32)).astype(out.dtype)


def project_kernel(kept, received, w_ref, _, projected, flipped):
    total = kept[...] + received[...].astype(F32)
    high = total.astype(BF16)
    low = (total - high.astype(F32)).astype(BF16)
    projected[...] = jnp.dot(high, w_ref[...], preferred_element_type=F32) + jnp.dot(
        low, w_ref[...], preferred_element_type=F32
    )
    flipped[...] = total.T.astype(BF16)


def add_pulls(pulls, held, code, tile_of, acc):
    for i, piece in pulls:
        block = piece[part(code[i] % held, BLK), :]
        rows = part(code[i] // held, BLK)
        acc[rows, :] += jnp.dot(tile_of(i), block, preferred_element_type=F32)


def pulls_of(chips, pieces):
    return [
        (i * CAP + m, piece)
        for i, piece in zip(chips, pieces, strict=True)
        for m in range(CAP)
    ]


def early_kernel(offsets, held, which, code, which2, code2, tiles, tiles2, *refs):
    pieces, (own, others) = refs[:-2], refs[-2:]
    pulls = pulls_of(offsets, pieces)
    own[...] = jnp.zeros_like(own)
    others[...] = jnp.zeros_like(others)
    add_pulls(pulls, held, code2, lambda i: tiles2[which2[i]], others)
    add_pulls(pulls, held, code, lambda i: tiles[which[i]], own)


def others_kernel(offsets, held, which, code, acc_in, tiles, _, *refs):
    pieces, (out, acc) = refs[:-2], refs[-2:]
    acc[...] = acc_in[...]
    add_pulls(pulls_of(offsets, pieces), held, code, lambda i: tiles[which[i]], acc)
    out[...] = acc[: out.shape[0], :].astype(BF16)


def own_kernel(offsets, held, which, code, acc_in, tiles, *refs):
    pieces, out = refs[:-1], refs[-1]
    out[...] = acc_in[...]
    add_pulls(pulls_of(offsets, pieces), held, code, lambda i: tiles[which[i]], out)


def merge_kernel(n_col, projected, own, received, keep, *sends):
    span = keep.shape[0]
    c = lax.axis_index("col")
    for s in range(n_col):
        rows = part(c ^ s, span)
        block = own[rows, :] + received[rows, :].astype(F32)
        if s:
            sends[s - 1][...] = block.astype(BF16)
        else:
            keep[...] = block + projected[...]


def gradient_kernel(cotangent, kept, *refs):
    parts, (mixed_out, flipped) = refs[:-2], refs[-2:]
    mixed = kept[...]
    for ref in parts:
        mixed = mixed + ref[...].astype(F32)
    mixed_out[...] = mixed
    sigmoid_z = jax.nn.sigmoid(mixed)
    grad_pre = cotangent[...].astype(F32) * sigmoid_z * (1.0 + mixed * (1.0 - sigmoid_z))
    flipped[...] = grad_pre.T.astype(BF16)


def activate_kernel(mixed, kept, received, activated, total):
    activated[...] = (mixed[...] * jax.nn.sigmoid(mixed[...])).astype(BF16)
    total[...] = (kept[...] + received[...].astype(F32)).astype(BF16)


def scale_kernel(scale, *refs):
    refs, out = refs[:-1], refs[-1]
    count, rows = len(refs) // 2, refs[0].shape[0]
    core = lax.axis_index("row") % 2
    for i, ref in enumerate(refs):
        at = core if i < count else 1 - core
        out[part(at * count + i % count, rows), :] = ref[...].astype(F32) * scale


def nodes_kernel(w_ref, *refs):
    refs, out = refs[:-1], refs[-1]
    total = refs[0][...]
    for ref in refs[1:]:
        total = total + ref[...].astype(F32)
    out[...] = lax.dot_general(
        total.T.astype(BF16), w_ref[...], (((1,), (1,)), ((), ())), preferred_element_type=F32
    ).astype(BF16)


def weight_kernel(x_ref, g_ref, kept, given):
    half = x_ref.shape[0] // 2
    mine = lax.axis_index("row") % 2
    for out, core in ((kept, mine), (given, 1 - mine)):
        product = lax.dot_general(
            x_ref[part(core, half), :],
            g_ref[...],
            (((1,), (1,)), ((), ())),
            preferred_element_type=F32,
        )
        out[...] = product.astype(out.dtype)


def panel_kernel(offsets, *refs):
    pieces, out = refs[:-1], refs[-1]
    span = pieces[0].shape[1]
    c = lax.axis_index("col")
    for s, piece in zip(offsets, pieces, strict=True):
        out[:, part(c ^ s, span)] = piece[...]


def transposed_kernel(offsets, a_ref, g_ref, _, given, kept):
    span = kept.shape[2]
    r = lax.axis_index("row")
    for out, core in ((given, 1), (kept, 0)):
        for i, t in enumerate(offsets):
            columns = part(r ^ t ^ core, span)
            product = jnp.dot(g_ref[...], a_ref[:, columns], preferred_element_type=F32)
            out[i] = product.astype(out.dtype)


def tree_kernel(*refs):
    terms, out = [ref[...].astype(F32) for ref in refs[:-2]], refs[-1]
    while len(terms) > 1:
        terms = [a + b for a, b in zip(terms[::2], terms[1::2], strict=True)]
    out[...] = terms[0].astype(out.dtype)


def cores_kernel(places, kept, received, _, *outs):
    for i, out in zip(places, outs, strict=True):
        out[...] = (kept[i] + received[i].astype(F32)).astype(out.dtype)


def reduce_columns(blocks, span, hid):
    bit, halved = 1, None
    while True:
        keep, send = blocks[::2], blocks[1::2]
        received = [swap(x, "col", bit) for x in send]
        count = len(keep)
        if count == 1:
            return keep[0], received[0], halved
        bit *= 2
        blocks = call(
            functools.partial(halve_kernel, count),
            [shape(span, hid, dtype=BF16 if s % 2 else F32) for s in range(count)],
            [*keep, *received],
        )
        halved = blocks[1]


def local(
    nodes, weight, adjacency, history, pull_owner, pull_slot, pull_target, hist_tiles, cotangent
):
    n_row, n_col = lax.axis_size("row"), lax.axis_size("col")
    span, hid = nodes.shape
    panel, columns = adjacency.shape
    row_count = panel // BLK
    chips = list(range(0, n_row, 2))
    offsets = column_offsets(n_col)

    pulls = jnp.stack([pull_owner[:, 0], pull_slot, pull_target])
    their_pulls = swap(pulls, "row", 1)
    tiles = swap(hist_tiles, "row", 1)

    beside = swap(nodes, "row", 1)
    near = [swap(nodes, "row", t) for t in chips[:0:-1]][::-1]
    (history,) = call(later_kernel, [shape(*history.shape)], [history, beside, tiles])
    stacked = call(
        stack_kernel, [shape(len(near), span // 2, hid)] * 2, [*near, history]
    )
    across = [swap(x, "row", 1) for x in stacked]

    blocks = call(
        functools.partial(aggregate_kernel, n_row, n_col),
        [shape(span, hid, dtype=BF16 if s % 2 else F32) for s in range(n_col)],
        [adjacency, nodes, beside, *near, *across],
        [shape(columns, hid)],
    )
    keep, received, halved = reduce_columns(blocks, span, hid)
    blocks_held = history.shape[0] // BLK
    places = len(chips) * CAP
    which, code, which2, code2 = pl.pallas_call(
        functools.partial(lists_kernel, blocks_held, row_count),
        out_shape=[shape(places, dtype=jnp.int32)] * 4,
        in_specs=[SCALARS] * 2 + [WHOLE],
        out_specs=[SCALARS] * 4,
        scratch_shapes=[pltpu.SMEM((n_row,), jnp.int32)],
        compiler_params=pltpu.CompilerParams(vmem_limit_bytes=4 << 20),
    )(pulls, their_pulls, halved)

    past = [history] + [swap(history, "row", t) for t in chips[1:]]
    early = [i for i, t in enumerate(chips) if t & (t - 1) == 0]
    late = [i for i, t in enumerate(chips) if t & (t - 1)]

    spare = shape(panel + BLK, hid, dtype=F32)
    own_terms, terms = call(
        functools.partial(early_kernel, early, blocks_held),
        [spare, spare],
        [hist_tiles, tiles, *[past[i] for i in early]],
        lists=[which, code, which2, code2],
    )
    projected, summed = call(
        project_kernel, [shape(span, hid, dtype=F32), shape(hid, span)], [keep, received, weight, own_terms]
    )
    (given,) = call(
        functools.partial(others_kernel, late, blocks_held),
        [shape(panel, hid)],
        [terms, tiles, projected, *[past[i] for i in late]],
        [spare],
        [which2, code2],
    )
    received = swap(given, "row", 1)
    (terms,) = call(
        functools.partial(own_kernel, late, blocks_held),
        [spare],
        [own_terms, hist_tiles, *[past[i] for i in late]],
        lists=[which, code],
    )
    keep, *sends = call(
        functools.partial(merge_kernel, n_col),
        [shape(span, hid, dtype=BF16 if s else F32) for s in range(n_col)],
        [projected, terms, received],
    )
    mixed, flipped = call(
        gradient_kernel,
        [shape(span, hid, dtype=F32), shape(hid, span)],
        [cotangent, keep, *[swap(sends[s - 1], "col", s) for s in offsets]],
    )

    pieces = [swap(flipped, "col", s) if s else flipped for s in [*offsets, 0]]
    kept, given = call(
        weight_kernel,
        [shape(hid // 2, hid, dtype=F32), shape(hid // 2, hid)],
        [summed, flipped],
    )
    activated, kept = call(
        activate_kernel,
        [shape(span, hid), shape(hid // 2, hid)],
        [mixed, kept, swap(given, "row", 1)],
    )
    gradients = call(
        functools.partial(panel_kernel, [*offsets, 0]), [shape(hid, panel)], pieces
    )[0]
    (halfway,) = call(
        tree_kernel,
        [shape(hid // 2, hid)],
        [*[swap(kept, "row", t) if t else kept for t in chips], gradients],
    )

    given, kept = call(
        functools.partial(transposed_kernel, chips),
        [shape(len(chips), hid, span, dtype=dtype) for dtype in (BF16, F32)],
        [adjacency, gradients, halfway],
    )
    received = swap(given, "row", 1)
    arrived, token = {}, given
    for places in (list(range(1, len(chips))), [0]):
        sums = call(
            functools.partial(cores_kernel, places),
            [shape(hid, span, dtype=BF16 if i else F32) for i in places],
            [kept, received, token],
        )
        for i, x in zip(places, sums, strict=True):
            arrived[i] = swap(x, "row", chips[i]) if i else x
        if token is given:
            beside = swap(halfway, "col", 1)
            (token,) = call(add_kernel, [shape(*halfway.shape)], [halfway, beside, sums[0]])
    halfway = token
    (grad_nodes,) = call(
        nodes_kernel, [shape(span, hid)], [weight, *[arrived[i] for i in range(len(chips))]]
    )

    halfway = [halfway]
    for bit in [1 << b for b in range(1, n_col.bit_length() - 1)]:
        received = swap(halfway[0], "col", bit)
        count = 2 if 2 * bit == n_col else 1
        halfway = call(
            add_kernel,
            [shape(hid // 2 // count, hid)] * count,
            [halfway[0], received, arrived[len(chips) - 1]],
        )
    scale = 1.0 / math.sqrt(span * n_row * n_col)
    (grad_weight,) = call(
        functools.partial(scale_kernel, scale),
        [shape(hid, hid, dtype=F32)],
        [*halfway, *[swap(x, "row", 1) for x in halfway]],
    )
    return (activated, grad_nodes, grad_weight)


def solution(mesh):
    return jax.shard_map(
        local,
        mesh=mesh,
        in_specs=(
            P(("row", "col"), None),
            P(),
            P("row", "col"),
            P(("row", "col"), None),
            P(("row", "col"), None),
            P(("row", "col")),
            P(("row", "col")),
            P(("row", "col"), None, None),
            P(("row", "col"), None),
        ),
        out_specs=(P(("row", "col"), None), P(("row", "col"), None), P()),
        check_vma=False,
    )
```

```python
import functools
import math

import jax
import jax.numpy as jnp
from jax import lax
from jax.experimental import pallas as pl
from jax.experimental.pallas import tpu as pltpu
from jax.sharding import PartitionSpec as P

BLK = 128
CAP = 4
BF16 = jnp.bfloat16
F32 = jnp.float32
WHOLE = pl.BlockSpec(memory_space=pltpu.VMEM)
SCALARS = pl.BlockSpec(memory_space=pltpu.SMEM)


def swap(x, axis, offset):
    size = lax.axis_size(axis)
    return lax.ppermute(x, axis, [(i, i ^ offset) for i in range(size)])


def shape(*dims, dtype=BF16):
    return jax.ShapeDtypeStruct(dims, dtype)


def column_offsets(n_col):
    return [n_col - 1, *range(1, n_col - 1)]


def nbytes(arrays):
    return sum(math.prod(a.shape) * jnp.dtype(a.dtype).itemsize for a in arrays)


def call(kernel, outs, operands, scratch=(), lists=()):
    held = nbytes(outs) + nbytes(scratch)
    operands = [pltpu.with_memory_space_constraint(x, pltpu.VMEM) for x in operands]
    return pl.pallas_call(
        kernel,
        out_shape=outs,
        in_specs=[SCALARS] * len(lists) + [WHOLE] * len(operands),
        out_specs=[WHOLE] * len(outs),
        scratch_shapes=[pltpu.VMEM(x.shape, x.dtype) for x in scratch],
        compiler_params=pltpu.CompilerParams(vmem_limit_bytes=held + (4 << 20)),
        cost_estimate=pl.CostEstimate(flops=0, bytes_accessed=0, transcendentals=0),
    )(*lists, *operands)


def part(index, size):
    return pl.ds(pl.multiple_of(index * size, size), size)


def later_kernel(x_ref, *refs):
    out = refs[-1]
    out[...] = x_ref[...]


def add_kernel(x_ref, y_ref, _, *outs):
    rows = outs[0].shape[0]
    for i, out in enumerate(outs):
        at = pl.ds(i * rows, rows)
        out[...] = (x_ref[at, :].astype(F32) + y_ref[at, :].astype(F32)).astype(out.dtype)


def stack_kernel(own, *refs):
    refs, (_, out) = refs[:-2], refs[-2:]
    span = own.shape[0]
    half = span // 2
    out[:half, :] = own[half:, :]
    for i, ref in enumerate(refs):
        out[pl.ds(half + i * span, span), :] = ref[...]


def lists_kernel(held, spare, mine, theirs, _, which, code, which2, code2, count):
    r = lax.axis_index("row")
    for refs in ((which, code), (which2, code2)):
        for i in range(refs[0].shape[0]):
            refs[0][i] = 0
            refs[1][i] = spare * held
    for t in range(count.shape[0]):
        count[t] = 0

    def place(k, _):
        for pulls, refs, at in (
            (mine, (which, code), 0),
            (theirs, (which2, code2), count.shape[0] // 2),
        ):
            t = pulls[0, k] ^ r

            @pl.when(t % 2 == 0)
            def _(pulls=pulls, refs=refs, at=at, t=t):
                chip = t // 2
                i = chip * CAP + count[at + chip]
                count[at + chip] += 1
                refs[0][i] = k
                refs[1][i] = pulls[2, k] * held + pulls[1, k]

        return 0

    lax.fori_loop(0, mine.shape[1], place, 0)


def aggregate_kernel(n_row, n_col, a_ref, own, other, *refs):
    near, (across, keep, send, x_ref) = refs[:-4], refs[-4:]
    span = own.shape[0]
    half = span // 2
    r, c = lax.axis_index("row"), lax.axis_index("col")
    x_ref[part(r, span), :] = own[...]
    x_ref[part(r ^ 1, span), :] = other[...]
    for i, ref in enumerate(near):
        t = 2 * (i + 1)
        x_ref[part(r ^ t, span), :] = ref[...]
        x_ref[part(r ^ t ^ 1, span), :] = across[pl.ds(half + i * span, span), :]
    for s in range(n_col):
        block = jnp.dot(a_ref[part(c ^ s, span), :], x_ref[...], preferred_element_type=F32)
        if s % 2:
            send[s // 2] = block.astype(BF16)
        else:
            keep[s // 2] = block


def halve_kernel(kept, received, keep, send):
    for i in range(kept.shape[0]):
        block = kept[i] + received[i].astype(F32)
        if i % 2:
            send[i // 2] = block.astype(BF16)
        else:
            keep[i // 2] = block


def project_kernel(kept, received, w_ref, _, projected, flipped):
    total = kept[0] + received[0].astype(F32)
    high = total.astype(BF16)
    low = (total - high.astype(F32)).astype(BF16)
    projected[...] = jnp.dot(high, w_ref[...], preferred_element_type=F32) + jnp.dot(
        low, w_ref[...], preferred_element_type=F32
    )
    flipped[...] = total.T.astype(BF16)


def add_pulls(pulls, held, code, tile_of, acc):
    half = held // 2
    for i, piece in pulls:
        slot = code[i] % held
        if len(piece) == 1:
            block = piece[0][part(slot, BLK), :]
        else:
            inside = part(slot % half, BLK)
            block = jnp.where(slot < half, piece[0][inside, :], piece[1][inside, :])
        rows = part(code[i] // held, BLK)
        acc[rows, :] += jnp.dot(tile_of(i), block, preferred_element_type=F32)


def slice_kernel(at, x_ref, out):
    out[...] = x_ref[pl.ds(at, out.shape[0]), :]


def pulls_of(chips, pieces):
    return [
        (i * CAP + m, piece)
        for i, piece in zip(chips, pieces, strict=True)
        for m in range(CAP)
    ]


def early_kernel(offsets, held, which, code, which2, code2, tiles, tiles2, *refs):
    pieces, (own, others) = [(ref,) for ref in refs[:-2]], refs[-2:]
    pulls = pulls_of(offsets, pieces)
    own[...] = jnp.zeros_like(own)
    others[...] = jnp.zeros_like(others)
    add_pulls(pulls, held, code2, lambda i: tiles2[which2[i]], others)
    add_pulls(pulls, held, code, lambda i: tiles[which[i]], own)


def others_kernel(offsets, held, count, which, code, acc_in, tiles, *refs):
    refs, outs, acc = refs[: -1 - count], refs[-1 - count : -1], refs[-1]
    pieces = list(zip(refs[::2], refs[1::2], strict=True))
    acc[...] = acc_in[...]
    add_pulls(pulls_of(offsets, pieces), held, code, lambda i: tiles[which[i]], acc)
    rows = outs[0].shape[0]
    for i, out in enumerate(outs):
        out[...] = acc[pl.ds(i * rows, rows), :].astype(BF16)


def own_kernel(offsets, held, which, code, acc_in, tiles, *refs):
    pieces, out = list(zip(refs[:-1:2], refs[1:-1:2], strict=True)), refs[-1]
    out[...] = acc_in[...]
    add_pulls(pulls_of(offsets, pieces), held, code, lambda i: tiles[which[i]], out)


def merge_kernel(n_col, projected, own, *refs):
    received, outs, acc = refs[:n_col], refs[n_col:-1], refs[-1]
    span = outs[0].shape[0]
    c = lax.axis_index("col")
    for i, ref in enumerate(received):
        rows = pl.ds(i * span, span)
        acc[rows, :] = own[rows, :] + ref[...].astype(F32)
    for s, out in enumerate(outs):
        block = acc[part(c ^ s, span), :]
        out[...] = block.astype(out.dtype) if s else block + projected[...]


def gradient_kernel(cotangent, kept, *refs):
    parts, (mixed_out, flipped) = refs[:-2], refs[-2:]
    mixed = kept[...]
    for ref in parts:
        mixed = mixed + ref[...].astype(F32)
    mixed_out[...] = mixed
    sigmoid_z = jax.nn.sigmoid(mixed)
    grad_pre = cotangent[...].astype(F32) * sigmoid_z * (1.0 + mixed * (1.0 - sigmoid_z))
    flipped[...] = grad_pre.T.astype(BF16)


def activate_kernel(mixed, kept, received, activated, total):
    activated[...] = (mixed[...] * jax.nn.sigmoid(mixed[...])).astype(BF16)
    total[...] = (kept[...] + received[...].astype(F32)).astype(BF16)


def scale_kernel(scale, *refs):
    refs, out = refs[:-1], refs[-1]
    count, rows = len(refs) // 2, refs[0].shape[0]
    core = lax.axis_index("row") % 2
    for i, ref in enumerate(refs):
        at = core if i < count else 1 - core
        out[part(at * count + i % count, rows), :] = ref[...].astype(F32) * scale


def nodes_kernel(w_ref, *refs):
    refs, out = refs[:-1], refs[-1]
    total = refs[0][...]
    for ref in refs[1:]:
        total = total + ref[...].astype(F32)
    out[...] = lax.dot_general(
        total.T.astype(BF16), w_ref[...], (((1,), (1,)), ((), ())), preferred_element_type=F32
    ).astype(BF16)


def weight_kernel(x_ref, g_ref, kept, given):
    half = x_ref.shape[0] // 2
    mine = lax.axis_index("row") % 2
    for out, core in ((kept, mine), (given, 1 - mine)):
        product = lax.dot_general(
            x_ref[part(core, half), :],
            g_ref[...],
            (((1,), (1,)), ((), ())),
            preferred_element_type=F32,
        )
        out[...] = product.astype(out.dtype)


def panel_kernel(offsets, *refs):
    pieces, out = refs[:-1], refs[-1]
    span = pieces[0].shape[1]
    c = lax.axis_index("col")
    for s, piece in zip(offsets, pieces, strict=True):
        out[:, part(c ^ s, span)] = piece[...]


def transposed_kernel(offsets, a_ref, g_ref, _, given, kept):
    span = kept.shape[2]
    r = lax.axis_index("row")
    for out, core in ((given, 1), (kept, 0)):
        for i, t in enumerate(offsets):
            columns = part(r ^ t ^ core, span)
            product = jnp.dot(g_ref[...], a_ref[:, columns], preferred_element_type=F32)
            out[i] = product.astype(out.dtype)


def tree_kernel(*refs):
    terms, out = [ref[...].astype(F32) for ref in refs[:-2]], refs[-1]
    while len(terms) > 1:
        terms = [a + b for a, b in zip(terms[::2], terms[1::2], strict=True)]
    out[...] = terms[0].astype(out.dtype)


def cores_kernel(places, kept, received, _, *outs):
    for i, out in zip(places, outs, strict=True):
        out[...] = (kept[i] + received[i].astype(F32)).astype(out.dtype)


def reduce_columns(keep, send):
    bit = 1
    while True:
        received = swap(send, "col", bit)
        count, span, hid = keep.shape
        if count == 1:
            return keep, received, send
        bit *= 2
        keep, send = call(
            halve_kernel,
            [shape(count // 2, span, hid, dtype=F32), shape(count // 2, span, hid)],
            [keep, received],
        )


def local(
    nodes, weight, adjacency, history, pull_owner, pull_slot, pull_target, hist_tiles, cotangent
):
    n_row, n_col = lax.axis_size("row"), lax.axis_size("col")
    span, hid = nodes.shape
    panel, columns = adjacency.shape
    row_count = panel // BLK
    chips = list(range(0, n_row, 2))
    offsets = column_offsets(n_col)

    pulls = jnp.stack([pull_owner[:, 0], pull_slot, pull_target])
    their_pulls = swap(pulls, "row", 1)
    tiles = swap(hist_tiles, "row", 1)

    beside = swap(nodes, "row", 1)
    near = [swap(nodes, "row", t) for t in chips[:0:-1]][::-1]
    (history,) = call(later_kernel, [shape(*history.shape)], [history, beside, tiles])
    (stacked,) = call(
        stack_kernel,
        [shape(span // 2 + len(near) * span, hid)],
        [nodes, *near, history],
    )
    across = swap(stacked, "row", 1)

    keep, send = call(
        functools.partial(aggregate_kernel, n_row, n_col),
        [shape(n_col // 2, span, hid, dtype=F32), shape(n_col // 2, span, hid)],
        [adjacency, nodes, beside, *near, across],
        [shape(columns, hid)],
    )
    keep, received, halved = reduce_columns(keep, send)

    blocks_held = history.shape[0] // BLK
    places = len(chips) * CAP
    which, code, which2, code2 = pl.pallas_call(
        functools.partial(lists_kernel, blocks_held, row_count),
        out_shape=[shape(places, dtype=jnp.int32)] * 4,
        in_specs=[SCALARS] * 2 + [WHOLE],
        out_specs=[SCALARS] * 4,
        scratch_shapes=[pltpu.SMEM((n_row,), jnp.int32)],
        compiler_params=pltpu.CompilerParams(vmem_limit_bytes=4 << 20),
    )(pulls, their_pulls, halved)

    middle = history.shape[0] // 2
    bits = [1 << b for b in range(1, n_row.bit_length() - 1)]
    past = {0: history, **{bit: swap(history, "row", bit) for bit in bits}}
    halves = []
    for at, order in ((0, bits), (middle, bits[::-1])):
        held = {}
        for bit in order:
            held.update({t ^ bit: swap(x, "row", bit) for t, x in list(held.items())})
            (held[bit],) = call(
                functools.partial(slice_kernel, at), [shape(middle, hid)], [past[bit]]
            )
        halves.append(held)
    early = [i for i, t in enumerate(chips) if t & (t - 1) == 0]
    late = [i for i, t in enumerate(chips) if t & (t - 1)]
    forwarded = [held[chips[i]] for i in late for held in halves]

    spare = shape(panel + BLK, hid, dtype=F32)
    own_terms, terms = call(
        functools.partial(early_kernel, early, blocks_held),
        [spare, spare],
        [hist_tiles, tiles, *[past[chips[i]] for i in early]],
        lists=[which, code, which2, code2],
    )
    projected, summed = call(
        project_kernel, [shape(span, hid, dtype=F32), shape(hid, span)], [keep, received, weight, own_terms]
    )
    given = call(
        functools.partial(others_kernel, late, blocks_held, n_col),
        [shape(span, hid)] * n_col,
        [terms, tiles, *forwarded],
        [spare],
        [which2, code2],
    )
    received = [swap(x, "row", 1) for x in given]
    (terms,) = call(
        functools.partial(own_kernel, late, blocks_held),
        [spare],
        [own_terms, hist_tiles, *forwarded],
        lists=[which, code],
    )
    keep, *sends = call(
        functools.partial(merge_kernel, n_col),
        [shape(span, hid, dtype=BF16 if s else F32) for s in range(n_col)],
        [projected, terms, *received],
        [shape(panel, hid, dtype=F32)],
    )
    mixed, flipped = call(
        gradient_kernel,
        [shape(span, hid, dtype=F32), shape(hid, span)],
        [cotangent, keep, *[swap(sends[s - 1], "col", s) for s in offsets]],
    )

    pieces = [swap(flipped, "col", s) if s else flipped for s in [*offsets, 0]]
    kept, given = call(
        weight_kernel,
        [shape(hid // 2, hid, dtype=F32), shape(hid // 2, hid)],
        [summed, flipped],
    )
    activated, kept = call(
        activate_kernel,
        [shape(span, hid), shape(hid // 2, hid)],
        [mixed, kept, swap(given, "row", 1)],
    )
    gradients = call(
        functools.partial(panel_kernel, [*offsets, 0]), [shape(hid, panel)], pieces
    )[0]
    (halfway,) = call(
        tree_kernel,
        [shape(hid // 2, hid)],
        [*[swap(kept, "row", t) if t else kept for t in chips], gradients],
    )

    given, kept = call(
        functools.partial(transposed_kernel, chips),
        [shape(len(chips), hid, span, dtype=dtype) for dtype in (BF16, F32)],
        [adjacency, gradients, halfway],
    )
    received = swap(given, "row", 1)
    arrived, token = {}, given
    for places in (list(range(1, len(chips))), [0]):
        sums = call(
            functools.partial(cores_kernel, places),
            [shape(hid, span, dtype=BF16 if i else F32) for i in places],
            [kept, received, token],
        )
        for i, x in zip(places, sums, strict=True):
            arrived[i] = swap(x, "row", chips[i]) if i else x
        if token is given:
            beside = swap(halfway, "col", 1)
            (token,) = call(add_kernel, [shape(*halfway.shape)], [halfway, beside, sums[0]])
    halfway = token
    (grad_nodes,) = call(
        nodes_kernel, [shape(span, hid)], [weight, *[arrived[i] for i in range(len(chips))]]
    )

    halfway = [halfway]
    for bit in [1 << b for b in range(1, n_col.bit_length() - 1)]:
        received = swap(halfway[0], "col", bit)
        count = 2 if 2 * bit == n_col else 1
        halfway = call(
            add_kernel,
            [shape(hid // 2 // count, hid)] * count,
            [halfway[0], received, arrived[len(chips) - 1]],
        )
    scale = 1.0 / math.sqrt(span * n_row * n_col)
    (grad_weight,) = call(
        functools.partial(scale_kernel, scale),
        [shape(hid, hid, dtype=F32)],
        [*halfway, *[swap(x, "row", 1) for x in halfway]],
    )
    return (activated, grad_nodes, grad_weight)


def solution(mesh):
    return jax.shard_map(
        local,
        mesh=mesh,
        in_specs=(
            P(("row", "col"), None),
            P(),
            P("row", "col"),
            P(("row", "col"), None),
            P(("row", "col"), None),
            P(("row", "col")),
            P(("row", "col")),
            P(("row", "col"), None, None),
            P(("row", "col"), None),
        ),
        out_specs=(P(("row", "col"), None), P(("row", "col"), None), P()),
        check_vma=False,
    )
```

```python
import functools
import math

import jax
import jax.numpy as jnp
from jax import lax
from jax.experimental import pallas as pl
from jax.experimental.pallas import tpu as pltpu
from jax.sharding import PartitionSpec as P

BLK = 128
CAP = 4
BF16 = jnp.bfloat16
F32 = jnp.float32
WHOLE = pl.BlockSpec(memory_space=pltpu.VMEM)
SCALARS = pl.BlockSpec(memory_space=pltpu.SMEM)


def swap(x, axis, offset):
    size = lax.axis_size(axis)
    return lax.ppermute(x, axis, [(i, i ^ offset) for i in range(size)])


def shape(*dims, dtype=BF16):
    return jax.ShapeDtypeStruct(dims, dtype)


def column_offsets(n_col):
    return [n_col - 1, *range(1, n_col - 1)]


def nbytes(arrays):
    return sum(math.prod(a.shape) * jnp.dtype(a.dtype).itemsize for a in arrays)


def call(kernel, outs, operands, scratch=(), lists=()):
    held = nbytes(outs) + nbytes(scratch)
    operands = [pltpu.with_memory_space_constraint(x, pltpu.VMEM) for x in operands]
    return pl.pallas_call(
        kernel,
        out_shape=outs,
        in_specs=[SCALARS] * len(lists) + [WHOLE] * len(operands),
        out_specs=[WHOLE] * len(outs),
        scratch_shapes=[pltpu.VMEM(x.shape, x.dtype) for x in scratch],
        compiler_params=pltpu.CompilerParams(vmem_limit_bytes=held + (4 << 20)),
        cost_estimate=pl.CostEstimate(flops=0, bytes_accessed=0, transcendentals=0),
    )(*lists, *operands)


def part(index, size):
    return pl.ds(pl.multiple_of(index * size, size), size)


def later_kernel(x_ref, *refs):
    refs[-1][...] = x_ref[...]


def add_kernel(x_ref, y_ref, _, *outs):
    rows = outs[0].shape[0]
    for i, out in enumerate(outs):
        at = pl.ds(i * rows, rows)
        out[...] = (x_ref[at, :].astype(F32) + y_ref[at, :].astype(F32)).astype(out.dtype)


def stack_kernel(own, *refs):
    refs, out = refs[:-3], refs[-1]
    span = own.shape[0]
    half = span // 2
    out[:half, :] = own[half:, :]
    for i, ref in enumerate(refs):
        out[pl.ds(half + i * span, span), :] = ref[...]


def lists_kernel(held, spare, mine, theirs, _, which, code, which2, code2, made, count):
    r = lax.axis_index("row")
    made[...] = jnp.zeros_like(made)
    for refs in ((which, code), (which2, code2)):
        for i in range(refs[0].shape[0]):
            refs[0][i] = 0
            refs[1][i] = spare * held
    for t in range(count.shape[0]):
        count[t] = 0

    def place(k, _):
        for pulls, refs, at in (
            (mine, (which, code), 0),
            (theirs, (which2, code2), count.shape[0] // 2),
        ):
            t = pulls[0, k] ^ r

            @pl.when(t % 2 == 0)
            def _(pulls=pulls, refs=refs, at=at, t=t):
                chip = t // 2
                i = chip * CAP + count[at + chip]
                count[at + chip] += 1
                refs[0][i] = k
                refs[1][i] = pulls[2, k] * held + pulls[1, k]

        return 0

    lax.fori_loop(0, mine.shape[1], place, 0, unroll=True)


def aggregate_kernel(n_row, n_col, a_ref, own, other, *refs):
    near, (across, keep, send, x_ref) = refs[:-4], refs[-4:]
    span = own.shape[0]
    half = span // 2
    r, c = lax.axis_index("row"), lax.axis_index("col")
    x_ref[part(r, span), :] = own[...]
    x_ref[part(r ^ 1, span), :] = other[...]
    for i, ref in enumerate(near):
        t = 2 * (i + 1)
        x_ref[part(r ^ t, span), :] = ref[...]
        x_ref[part(r ^ t ^ 1, span), :] = across[pl.ds(half + i * span, span), :]
    for s in range(n_col):
        block = jnp.dot(a_ref[part(c ^ s, span), :], x_ref[...], preferred_element_type=F32)
        if s % 2:
            send[s // 2] = block.astype(BF16)
        else:
            keep[s // 2] = block


def halve_kernel(kept, received, keep, send):
    for i in range(kept.shape[0]):
        block = kept[i] + received[i].astype(F32)
        if i % 2:
            send[i // 2] = block.astype(BF16)
        else:
            keep[i // 2] = block


def project_kernel(kept, received, w_ref, _, projected, flipped):
    total = kept[0] + received[0].astype(F32)
    high = total.astype(BF16)
    low = (total - high.astype(F32)).astype(BF16)
    projected[...] = jnp.dot(high, w_ref[...], preferred_element_type=F32) + jnp.dot(
        low, w_ref[...], preferred_element_type=F32
    )
    flipped[...] = total.T.astype(BF16)


def add_pulls(pulls, held, code, tile_of, acc):
    half = held // 2
    for i, piece in pulls:
        slot = code[i] % held
        if len(piece) == 1:
            block = piece[0][part(slot, BLK), :]
        else:
            inside = part(slot % half, BLK)
            block = jnp.where(slot < half, piece[0][inside, :], piece[1][inside, :])
        rows = part(code[i] // held, BLK)
        acc[rows, :] += jnp.dot(tile_of(i), block, preferred_element_type=F32)


def slice_kernel(at, x_ref, out):
    out[...] = x_ref[pl.ds(at, out.shape[0]), :]


def pulls_of(chips, pieces):
    return [
        (i * CAP + m, piece)
        for i, piece in zip(chips, pieces, strict=True)
        for m in range(CAP)
    ]


def early_kernel(offsets, held, which, code, which2, code2, tiles, tiles2, *refs):
    pieces, (own, others) = [(ref,) for ref in refs[:-2]], refs[-2:]
    pulls = pulls_of(offsets, pieces)
    own[...] = jnp.zeros_like(own)
    others[...] = jnp.zeros_like(others)
    add_pulls(pulls, held, code2, lambda i: tiles2[which2[i]], others)
    add_pulls(pulls, held, code, lambda i: tiles[which[i]], own)


def others_kernel(offsets, held, count, which, code, acc_in, tiles, *refs):
    refs, outs, acc = refs[: -1 - count], refs[-1 - count : -1], refs[-1]
    pieces = list(zip(refs[::2], refs[1::2], strict=True))
    acc[...] = acc_in[...]
    add_pulls(pulls_of(offsets, pieces), held, code, lambda i: tiles[which[i]], acc)
    rows = outs[0].shape[0]
    for i, out in enumerate(outs):
        out[...] = acc[pl.ds(i * rows, rows), :].astype(BF16)


def own_kernel(offsets, held, which, code, acc_in, tiles, *refs):
    pieces, out = list(zip(refs[:-1:2], refs[1:-1:2], strict=True)), refs[-1]
    out[...] = acc_in[...]
    add_pulls(pulls_of(offsets, pieces), held, code, lambda i: tiles[which[i]], out)


def merge_kernel(n_col, projected, own, *refs):
    received, outs, acc = refs[:n_col], refs[n_col:-1], refs[-1]
    span = outs[0].shape[0]
    c = lax.axis_index("col")
    for i, ref in enumerate(received):
        rows = pl.ds(i * span, span)
        acc[rows, :] = own[rows, :] + ref[...].astype(F32)
    for s, out in enumerate(outs):
        block = acc[part(c ^ s, span), :]
        out[...] = block.astype(out.dtype) if s else block + projected[...]


def gradient_kernel(cotangent, kept, *refs):
    parts, (mixed_out, flipped) = refs[:-2], refs[-2:]
    mixed = kept[...]
    for ref in parts:
        mixed = mixed + ref[...].astype(F32)
    mixed_out[...] = mixed
    sigmoid_z = jax.nn.sigmoid(mixed)
    grad_pre = cotangent[...].astype(F32) * sigmoid_z * (1.0 + mixed * (1.0 - sigmoid_z))
    flipped[...] = grad_pre.T.astype(BF16)


def activate_kernel(mixed, kept, received, activated, total):
    activated[...] = (mixed[...] * jax.nn.sigmoid(mixed[...])).astype(BF16)
    total[...] = (kept[...] + received[...].astype(F32)).astype(BF16)


def scale_kernel(scale, *refs):
    refs, out = refs[:-1], refs[-1]
    count, rows = len(refs) // 2, refs[0].shape[0]
    core = lax.axis_index("row") % 2
    for i, ref in enumerate(refs):
        at = core if i < count else 1 - core
        out[part(at * count + i % count, rows), :] = ref[...].astype(F32) * scale


def nodes_kernel(w_ref, *refs):
    refs, out = refs[:-1], refs[-1]
    total = refs[0][...]
    for ref in refs[1:]:
        total = total + ref[...].astype(F32)
    out[...] = lax.dot_general(
        total.T.astype(BF16), w_ref[...], (((1,), (1,)), ((), ())), preferred_element_type=F32
    ).astype(BF16)


def weight_kernel(x_ref, g_ref, kept, given):
    half = x_ref.shape[0] // 2
    mine = lax.axis_index("row") % 2
    for out, core in ((kept, mine), (given, 1 - mine)):
        product = lax.dot_general(
            x_ref[part(core, half), :],
            g_ref[...],
            (((1,), (1,)), ((), ())),
            preferred_element_type=F32,
        )
        out[...] = product.astype(out.dtype)


def panel_kernel(offsets, *refs):
    pieces, out = refs[:-1], refs[-1]
    span = pieces[0].shape[1]
    c = lax.axis_index("col")
    for s, piece in zip(offsets, pieces, strict=True):
        out[:, part(c ^ s, span)] = piece[...]


def transposed_kernel(offsets, a_ref, g_ref, _, given, kept):
    span = kept.shape[2]
    r = lax.axis_index("row")
    for out, core in ((given, 1), (kept, 0)):
        for i, t in enumerate(offsets):
            columns = part(r ^ t ^ core, span)
            product = jnp.dot(g_ref[...], a_ref[:, columns], preferred_element_type=F32)
            out[i] = product.astype(out.dtype)


def tree_kernel(*refs):
    terms, out = [ref[...].astype(F32) for ref in refs[:-2]], refs[-1]
    while len(terms) > 1:
        terms = [a + b for a, b in zip(terms[::2], terms[1::2], strict=True)]
    out[...] = terms[0].astype(out.dtype)


def cores_kernel(places, kept, received, _, *outs):
    for i, out in zip(places, outs, strict=True):
        out[...] = (kept[i] + received[i].astype(F32)).astype(out.dtype)


def reduce_columns(keep, send):
    bit = 1
    while True:
        received = swap(send, "col", bit)
        count, span, hid = keep.shape
        if count == 1:
            return keep, received, send
        bit *= 2
        keep, send = call(
            halve_kernel,
            [shape(count // 2, span, hid, dtype=F32), shape(count // 2, span, hid)],
            [keep, received],
        )


def local(
    nodes, weight, adjacency, history, pull_owner, pull_slot, pull_target, hist_tiles, cotangent
):
    n_row, n_col = lax.axis_size("row"), lax.axis_size("col")
    span, hid = nodes.shape
    panel, columns = adjacency.shape
    row_count = panel // BLK
    chips = list(range(0, n_row, 2))
    offsets = column_offsets(n_col)

    pulls = jnp.stack([pull_owner[:, 0], pull_slot, pull_target])
    their_pulls = swap(pulls, "row", 1)
    tiles = swap(hist_tiles, "row", 1)

    beside = swap(nodes, "row", 1)
    near = [swap(nodes, "row", t) for t in chips[:0:-1]][::-1]
    (history,) = call(later_kernel, [shape(*history.shape)], [history, beside, tiles])
    blocks_held = history.shape[0] // BLK
    places = len(chips) * CAP
    which, code, which2, code2, made = pl.pallas_call(
        functools.partial(lists_kernel, blocks_held, row_count),
        out_shape=[shape(places, dtype=jnp.int32)] * 4 + [shape(8, 128, dtype=F32)],
        in_specs=[SCALARS] * 2 + [WHOLE],
        out_specs=[SCALARS] * 4 + [WHOLE],
        scratch_shapes=[pltpu.SMEM((n_row,), jnp.int32)],
        compiler_params=pltpu.CompilerParams(vmem_limit_bytes=4 << 20),
    )(pulls, their_pulls, history)

    (stacked,) = call(
        stack_kernel,
        [shape(span // 2 + len(near) * span, hid)],
        [nodes, *near, history, made],
    )
    across = swap(stacked, "row", 1)

    keep, send = call(
        functools.partial(aggregate_kernel, n_row, n_col),
        [shape(n_col // 2, span, hid, dtype=F32), shape(n_col // 2, span, hid)],
        [adjacency, nodes, beside, *near, across],
        [shape(columns, hid)],
    )
    keep, received, halved = reduce_columns(keep, send)

    middle = history.shape[0] // 2
    bits = [1 << b for b in range(1, n_row.bit_length() - 1)]
    past = {0: history, **{bit: swap(history, "row", bit) for bit in bits}}
    halves = []
    for at, order in ((0, bits), (middle, bits[::-1])):
        held = {}
        for bit in order:
            held.update({t ^ bit: swap(x, "row", bit) for t, x in list(held.items())})
            (held[bit],) = call(
                functools.partial(slice_kernel, at), [shape(middle, hid)], [past[bit]]
            )
        halves.append(held)
    early = [i for i, t in enumerate(chips) if t & (t - 1) == 0]
    late = [i for i, t in enumerate(chips) if t & (t - 1)]
    forwarded = [held[chips[i]] for i in late for held in halves]

    spare = shape(panel + BLK, hid, dtype=F32)
    own_terms, terms = call(
        functools.partial(early_kernel, early, blocks_held),
        [spare, spare],
        [hist_tiles, tiles, *[past[chips[i]] for i in early]],
        lists=[which, code, which2, code2],
    )
    projected, summed = call(
        project_kernel, [shape(span, hid, dtype=F32), shape(hid, span)], [keep, received, weight, own_terms]
    )
    given = call(
        functools.partial(others_kernel, late, blocks_held, n_col),
        [shape(span, hid)] * n_col,
        [terms, tiles, *forwarded],
        [spare],
        [which2, code2],
    )
    received = [swap(x, "row", 1) for x in given]
    (terms,) = call(
        functools.partial(own_kernel, late, blocks_held),
        [spare],
        [own_terms, hist_tiles, *forwarded],
        lists=[which, code],
    )
    keep, *sends = call(
        functools.partial(merge_kernel, n_col),
        [shape(span, hid, dtype=BF16 if s else F32) for s in range(n_col)],
        [projected, terms, *received],
        [shape(panel, hid, dtype=F32)],
    )
    mixed, flipped = call(
        gradient_kernel,
        [shape(span, hid, dtype=F32), shape(hid, span)],
        [cotangent, keep, *[swap(sends[s - 1], "col", s) for s in offsets]],
    )

    pieces = [swap(flipped, "col", s) if s else flipped for s in [*offsets, 0]]
    kept, given = call(
        weight_kernel,
        [shape(hid // 2, hid, dtype=F32), shape(hid // 2, hid)],
        [summed, flipped],
    )
    activated, kept = call(
        activate_kernel,
        [shape(span, hid), shape(hid // 2, hid)],
        [mixed, kept, swap(given, "row", 1)],
    )
    gradients = call(
        functools.partial(panel_kernel, [*offsets, 0]), [shape(hid, panel)], pieces
    )[0]
    (halfway,) = call(
        tree_kernel,
        [shape(hid // 2, hid)],
        [*[swap(kept, "row", t) if t else kept for t in chips], gradients],
    )

    given, kept = call(
        functools.partial(transposed_kernel, chips),
        [shape(len(chips), hid, span, dtype=dtype) for dtype in (BF16, F32)],
        [adjacency, gradients, halfway],
    )
    received = swap(given, "row", 1)
    arrived, token = {}, given
    for places in (list(range(1, len(chips))), [0]):
        sums = call(
            functools.partial(cores_kernel, places),
            [shape(hid, span, dtype=BF16 if i else F32) for i in places],
            [kept, received, token],
        )
        for i, x in zip(places, sums, strict=True):
            arrived[i] = swap(x, "row", chips[i]) if i else x
        if token is given:
            beside = swap(halfway, "col", 1)
            (token,) = call(add_kernel, [shape(*halfway.shape)], [halfway, beside, sums[0]])
    halfway = token
    (grad_nodes,) = call(
        nodes_kernel, [shape(span, hid)], [weight, *[arrived[i] for i in range(len(chips))]]
    )

    halfway = [halfway]
    for bit in [1 << b for b in range(1, n_col.bit_length() - 1)]:
        received = swap(halfway[0], "col", bit)
        count = 2 if 2 * bit == n_col else 1
        halfway = call(
            add_kernel,
            [shape(hid // 2 // count, hid)] * count,
            [halfway[0], received, arrived[len(chips) - 1]],
        )
    scale = 1.0 / math.sqrt(span * n_row * n_col)
    (grad_weight,) = call(
        functools.partial(scale_kernel, scale),
        [shape(hid, hid, dtype=F32)],
        [*halfway, *[swap(x, "row", 1) for x in halfway]],
    )
    return (activated, grad_nodes, grad_weight)


def solution(mesh):
    return jax.shard_map(
        local,
        mesh=mesh,
        in_specs=(
            P(("row", "col"), None),
            P(),
            P("row", "col"),
            P(("row", "col"), None),
            P(("row", "col"), None),
            P(("row", "col")),
            P(("row", "col")),
            P(("row", "col"), None, None),
            P(("row", "col"), None),
        ),
        out_specs=(P(("row", "col"), None), P(("row", "col"), None), P()),
        check_vma=False,
    )
```

```python
import functools
import math

import jax
import jax.numpy as jnp
from jax import lax
from jax.experimental import pallas as pl
from jax.experimental.pallas import tpu as pltpu
from jax.sharding import PartitionSpec as P

BLK = 128
CAP = 4
BF16 = jnp.bfloat16
F32 = jnp.float32
WHOLE = pl.BlockSpec(memory_space=pltpu.VMEM)
SCALARS = pl.BlockSpec(memory_space=pltpu.SMEM)


def swap(x, axis, offset):
    size = lax.axis_size(axis)
    return lax.ppermute(x, axis, [(i, i ^ offset) for i in range(size)])


def shape(*dims, dtype=BF16):
    return jax.ShapeDtypeStruct(dims, dtype)


def column_offsets(n_col):
    return [n_col - 1, *range(1, n_col - 1)]


def nbytes(arrays):
    return sum(math.prod(a.shape) * jnp.dtype(a.dtype).itemsize for a in arrays)


def call(kernel, outs, operands, scratch=(), lists=()):
    held = nbytes(outs) + nbytes(scratch)
    operands = [pltpu.with_memory_space_constraint(x, pltpu.VMEM) for x in operands]
    return pl.pallas_call(
        kernel,
        out_shape=outs,
        in_specs=[SCALARS] * len(lists) + [WHOLE] * len(operands),
        out_specs=[WHOLE] * len(outs),
        scratch_shapes=[pltpu.VMEM(x.shape, x.dtype) for x in scratch],
        compiler_params=pltpu.CompilerParams(vmem_limit_bytes=held + (4 << 20)),
        cost_estimate=pl.CostEstimate(flops=0, bytes_accessed=0, transcendentals=0),
    )(*lists, *operands)


def part(index, size):
    return pl.ds(pl.multiple_of(index * size, size), size)


def later_kernel(x_ref, *refs):
    refs[-1][...] = x_ref[...]


def add_kernel(x_ref, y_ref, _, *outs):
    rows = outs[0].shape[0]
    for i, out in enumerate(outs):
        at = pl.ds(i * rows, rows)
        out[...] = (x_ref[at, :].astype(F32) + y_ref[at, :].astype(F32)).astype(out.dtype)


def stack_kernel(own, *refs):
    refs, out = refs[:-3], refs[-1]
    span = own.shape[0]
    half = span // 2
    out[:half, :] = own[half:, :]
    for i, ref in enumerate(refs):
        out[pl.ds(half + i * span, span), :] = ref[...]


def lists_kernel(held, spare, mine, theirs, _, code, code2, made, count):
    pulls_held = mine.shape[1]
    r = lax.axis_index("row")
    made[...] = jnp.zeros_like(made)
    for ref in (code, code2):
        for i in range(ref.shape[0]):
            ref[i] = spare * held * pulls_held
    for t in range(count.shape[0]):
        count[t] = 0

    def place(k, _):
        for pulls, ref, at in (
            (mine, code, 0),
            (theirs, code2, count.shape[0] // 2),
        ):
            t = pulls[0, k] ^ r

            @pl.when(t % 2 == 0)
            def _(pulls=pulls, ref=ref, at=at, t=t):
                chip = t // 2
                i = chip * CAP + count[at + chip]
                count[at + chip] += 1
                ref[i] = (pulls[2, k] * held + pulls[1, k]) * pulls_held + k

        return 0

    lax.fori_loop(0, mine.shape[1], place, 0, unroll=True)


def aggregate_kernel(n_row, n_col, a_ref, own, other, *refs):
    near, (across, keep, send, x_ref) = refs[:-4], refs[-4:]
    span = own.shape[0]
    half = span // 2
    r, c = lax.axis_index("row"), lax.axis_index("col")
    x_ref[part(r, span), :] = own[...]
    x_ref[part(r ^ 1, span), :] = other[...]
    for i, ref in enumerate(near):
        t = 2 * (i + 1)
        x_ref[part(r ^ t, span), :] = ref[...]
        x_ref[part(r ^ t ^ 1, span), :] = across[pl.ds(half + i * span, span), :]
    for s in range(n_col):
        block = jnp.dot(a_ref[part(c ^ s, span), :], x_ref[...], preferred_element_type=F32)
        if s % 2:
            send[s // 2] = block.astype(BF16)
        else:
            keep[s // 2] = block


def halve_kernel(kept, received, keep, send):
    for i in range(kept.shape[0]):
        block = kept[i] + received[i].astype(F32)
        if i % 2:
            send[i // 2] = block.astype(BF16)
        else:
            keep[i // 2] = block


def add_pulls(pulls, held, code, tiles, acc):
    half, pulls_held = held // 2, tiles.shape[0]
    for i, piece in pulls:
        k, where = code[i] % pulls_held, code[i] // pulls_held
        slot = where % held
        if len(piece) == 1:
            block = piece[0][part(slot, BLK), :]
        else:
            inside = part(slot % half, BLK)
            block = jnp.where(slot < half, piece[0][inside, :], piece[1][inside, :])
        rows = part(where // held, BLK)
        acc[rows, :] += jnp.dot(tiles[k], block, preferred_element_type=F32)


def slice_kernel(at, x_ref, out):
    out[...] = x_ref[pl.ds(at, out.shape[0]), :]


def pulls_of(chips, pieces):
    return [
        (i * CAP + m, piece)
        for i, piece in zip(chips, pieces, strict=True)
        for m in range(CAP)
    ]


def early_kernel(offsets, held, code, code2, tiles, tiles2, *refs):
    pieces, (own, others) = [(ref,) for ref in refs[:-2]], refs[-2:]
    pulls = pulls_of(offsets, pieces)
    own[...] = jnp.zeros_like(own)
    others[...] = jnp.zeros_like(others)
    add_pulls(pulls, held, code2, tiles2, others)
    add_pulls(pulls, held, code, tiles, own)


def others_kernel(offsets, held, count, code, acc_in, tiles, *refs):
    refs, outs, acc = refs[: -1 - count], refs[-1 - count : -1], refs[-1]
    pieces = list(zip(refs[::2], refs[1::2], strict=True))
    acc[...] = acc_in[...]
    add_pulls(pulls_of(offsets, pieces), held, code, tiles, acc)
    rows = outs[0].shape[0]
    for i, out in enumerate(outs):
        out[...] = acc[pl.ds(i * rows, rows), :].astype(BF16)


def own_kernel(offsets, held, code, acc_in, tiles, *refs):
    pieces, out = list(zip(refs[:-1:2], refs[1:-1:2], strict=True)), refs[-1]
    out[...] = acc_in[...]
    add_pulls(pulls_of(offsets, pieces), held, code, tiles, out)


def merge_kernel(n_col, kept, summed, w_ref, own, *refs):
    received, outs, (flipped, acc) = refs[:n_col], refs[n_col:-2], refs[-2:]
    span = outs[0].shape[0]
    c = lax.axis_index("col")
    for i, ref in enumerate(received):
        rows = pl.ds(i * span, span)
        acc[rows, :] = own[rows, :] + ref[...].astype(F32)
    for s, out in enumerate(outs[1:], 1):
        out[...] = acc[part(c ^ s, span), :].astype(out.dtype)
    total = kept[0] + summed[0].astype(F32)
    high = total.astype(BF16)
    low = (total - high.astype(F32)).astype(BF16)
    outs[0][...] = (
        acc[part(c, span), :]
        + jnp.dot(high, w_ref[...], preferred_element_type=F32)
        + jnp.dot(low, w_ref[...], preferred_element_type=F32)
    )
    flipped[...] = total.T.astype(BF16)


def gradient_kernel(cotangent, kept, *refs):
    parts, (mixed_out, flipped) = refs[:-2], refs[-2:]
    mixed = kept[...]
    for ref in parts:
        mixed = mixed + ref[...].astype(F32)
    mixed_out[...] = mixed
    sigmoid_z = jax.nn.sigmoid(mixed)
    grad_pre = cotangent[...].astype(F32) * sigmoid_z * (1.0 + mixed * (1.0 - sigmoid_z))
    flipped[...] = grad_pre.T.astype(BF16)


def activate_kernel(mixed, kept, received, activated, total):
    activated[...] = (mixed[...] * jax.nn.sigmoid(mixed[...])).astype(BF16)
    total[...] = (kept[...] + received[...].astype(F32)).astype(BF16)


def scale_kernel(scale, *refs):
    refs, out = refs[:-1], refs[-1]
    count, rows = len(refs) // 2, refs[0].shape[0]
    core = lax.axis_index("row") % 2
    for i, ref in enumerate(refs):
        at = core if i < count else 1 - core
        out[part(at * count + i % count, rows), :] = ref[...].astype(F32) * scale


def nodes_kernel(w_ref, *refs):
    refs, out = refs[:-1], refs[-1]
    total = refs[0][...]
    for ref in refs[1:]:
        total = total + ref[...].astype(F32)
    out[...] = lax.dot_general(
        total.T.astype(BF16), w_ref[...], (((1,), (1,)), ((), ())), preferred_element_type=F32
    ).astype(BF16)


def weight_kernel(x_ref, g_ref, kept, given):
    half = x_ref.shape[0] // 2
    mine = lax.axis_index("row") % 2
    for out, core in ((kept, mine), (given, 1 - mine)):
        product = lax.dot_general(
            x_ref[part(core, half), :],
            g_ref[...],
            (((1,), (1,)), ((), ())),
            preferred_element_type=F32,
        )
        out[...] = product.astype(out.dtype)


def panel_kernel(offsets, *refs):
    pieces, out = refs[:-1], refs[-1]
    span = pieces[0].shape[1]
    c = lax.axis_index("col")
    for s, piece in zip(offsets, pieces, strict=True):
        out[:, part(c ^ s, span)] = piece[...]


def transposed_kernel(offsets, a_ref, g_ref, _, given, kept):
    span = kept.shape[2]
    r = lax.axis_index("row")
    for out, core in ((given, 1), (kept, 0)):
        for i, t in enumerate(offsets):
            columns = part(r ^ t ^ core, span)
            product = jnp.dot(g_ref[...], a_ref[:, columns], preferred_element_type=F32)
            out[i] = product.astype(out.dtype)


def tree_kernel(*refs):
    terms, out = [ref[...].astype(F32) for ref in refs[:-2]], refs[-1]
    while len(terms) > 1:
        terms = [a + b for a, b in zip(terms[::2], terms[1::2], strict=True)]
    out[...] = terms[0].astype(out.dtype)


def cores_kernel(places, kept, received, _, *outs):
    for i, out in zip(places, outs, strict=True):
        out[...] = (kept[i] + received[i].astype(F32)).astype(out.dtype)


def reduce_columns(keep, send):
    bit = 1
    while True:
        received = swap(send, "col", bit)
        count, span, hid = keep.shape
        if count == 1:
            return keep, received, send
        bit *= 2
        keep, send = call(
            halve_kernel,
            [shape(count // 2, span, hid, dtype=F32), shape(count // 2, span, hid)],
            [keep, received],
        )


def local(
    nodes, weight, adjacency, history, pull_owner, pull_slot, pull_target, hist_tiles, cotangent
):
    n_row, n_col = lax.axis_size("row"), lax.axis_size("col")
    span, hid = nodes.shape
    panel, columns = adjacency.shape
    row_count = panel // BLK
    chips = list(range(0, n_row, 2))
    offsets = column_offsets(n_col)

    pulls = jnp.stack([pull_owner[:, 0], pull_slot, pull_target])
    their_pulls = swap(pulls, "row", 1)
    tiles = swap(hist_tiles, "row", 1)

    beside = swap(nodes, "row", 1)
    near = [swap(nodes, "row", t) for t in chips[:0:-1]][::-1]
    (history,) = call(later_kernel, [shape(*history.shape)], [history, beside, tiles])
    blocks_held = history.shape[0] // BLK
    places = len(chips) * CAP
    code, code2, made = pl.pallas_call(
        functools.partial(lists_kernel, blocks_held, row_count),
        out_shape=[shape(places, dtype=jnp.int32)] * 2 + [shape(8, 128, dtype=F32)],
        in_specs=[SCALARS] * 2 + [WHOLE],
        out_specs=[SCALARS] * 2 + [WHOLE],
        scratch_shapes=[pltpu.SMEM((n_row,), jnp.int32)],
        compiler_params=pltpu.CompilerParams(vmem_limit_bytes=4 << 20),
    )(pulls, their_pulls, history)

    (stacked,) = call(
        stack_kernel,
        [shape(span // 2 + len(near) * span, hid)],
        [nodes, *near, history, made],
    )
    across = swap(stacked, "row", 1)

    keep, send = call(
        functools.partial(aggregate_kernel, n_row, n_col),
        [shape(n_col // 2, span, hid, dtype=F32), shape(n_col // 2, span, hid)],
        [adjacency, nodes, beside, *near, across],
        [shape(columns, hid)],
    )
    keep, summed, halved = reduce_columns(keep, send)

    middle = history.shape[0] // 2
    bits = [1 << b for b in range(1, n_row.bit_length() - 1)]
    past = {0: history, **{bit: swap(history, "row", bit) for bit in bits}}
    halves = []
    for at, order in ((0, bits), (middle, bits[::-1])):
        held = {}
        for bit in order:
            held.update({t ^ bit: swap(x, "row", bit) for t, x in list(held.items())})
            (held[bit],) = call(
                functools.partial(slice_kernel, at), [shape(middle, hid)], [past[bit]]
            )
        halves.append(held)
    early = [i for i, t in enumerate(chips) if t & (t - 1) == 0]
    late = [i for i, t in enumerate(chips) if t & (t - 1)]
    forwarded = [held[chips[i]] for i in late for held in halves]

    spare = shape(panel + BLK, hid, dtype=F32)
    own_terms, terms = call(
        functools.partial(early_kernel, early, blocks_held),
        [spare, spare],
        [hist_tiles, tiles, *[past[chips[i]] for i in early]],
        lists=[code, code2],
    )
    given = call(
        functools.partial(others_kernel, late, blocks_held, n_col),
        [shape(span, hid)] * n_col,
        [terms, tiles, *forwarded],
        [spare],
        [code2],
    )
    received = [swap(x, "row", 1) for x in given]
    (terms,) = call(
        functools.partial(own_kernel, late, blocks_held),
        [spare],
        [own_terms, hist_tiles, *forwarded],
        lists=[code],
    )
    *blocks, summed = call(
        functools.partial(merge_kernel, n_col),
        [shape(span, hid, dtype=BF16 if s else F32) for s in range(n_col)] + [shape(hid, span)],
        [keep, summed, weight, terms, *received],
        [shape(panel, hid, dtype=F32)],
    )
    keep, *sends = blocks
    mixed, flipped = call(
        gradient_kernel,
        [shape(span, hid, dtype=F32), shape(hid, span)],
        [cotangent, keep, *[swap(sends[s - 1], "col", s) for s in offsets]],
    )

    pieces = [swap(flipped, "col", s) if s else flipped for s in [*offsets, 0]]
    kept, given = call(
        weight_kernel,
        [shape(hid // 2, hid, dtype=F32), shape(hid // 2, hid)],
        [summed, flipped],
    )
    activated, kept = call(
        activate_kernel,
        [shape(span, hid), shape(hid // 2, hid)],
        [mixed, kept, swap(given, "row", 1)],
    )
    gradients = call(
        functools.partial(panel_kernel, [*offsets, 0]), [shape(hid, panel)], pieces
    )[0]
    (halfway,) = call(
        tree_kernel,
        [shape(hid // 2, hid)],
        [*[swap(kept, "row", t) if t else kept for t in chips], gradients],
    )

    given, kept = call(
        functools.partial(transposed_kernel, chips),
        [shape(len(chips), hid, span, dtype=dtype) for dtype in (BF16, F32)],
        [adjacency, gradients, halfway],
    )
    received = swap(given, "row", 1)
    arrived, token = {}, given
    for places in (list(range(1, len(chips))), [0]):
        sums = call(
            functools.partial(cores_kernel, places),
            [shape(hid, span, dtype=BF16 if i else F32) for i in places],
            [kept, received, token],
        )
        for i, x in zip(places, sums, strict=True):
            arrived[i] = swap(x, "row", chips[i]) if i else x
        if token is given:
            beside = swap(halfway, "col", n_col // 2)
            (token,) = call(add_kernel, [shape(*halfway.shape)], [halfway, beside, sums[0]])
    halfway = token
    (grad_nodes,) = call(
        nodes_kernel, [shape(span, hid)], [weight, *[arrived[i] for i in range(len(chips))]]
    )

    halfway = [halfway]
    for bit in [1 << b for b in range(n_col.bit_length() - 2)][::-1]:
        received = swap(halfway[0], "col", bit)
        count = 2 if bit == 1 else 1
        halfway = call(
            add_kernel,
            [shape(hid // 2 // count, hid)] * count,
            [halfway[0], received, arrived[len(chips) - 1]],
        )
    scale = 1.0 / math.sqrt(span * n_row * n_col)
    (grad_weight,) = call(
        functools.partial(scale_kernel, scale),
        [shape(hid, hid, dtype=F32)],
        [*halfway, *[swap(x, "row", 1) for x in halfway]],
    )
    return (activated, grad_nodes, grad_weight)


def solution(mesh):
    return jax.shard_map(
        local,
        mesh=mesh,
        in_specs=(
            P(("row", "col"), None),
            P(),
            P("row", "col"),
            P(("row", "col"), None),
            P(("row", "col"), None),
            P(("row", "col")),
            P(("row", "col")),
            P(("row", "col"), None, None),
            P(("row", "col"), None),
        ),
        out_specs=(P(("row", "col"), None), P(("row", "col"), None), P()),
        check_vma=False,
    )
```

```python
import functools
import math

import jax
import jax.numpy as jnp
from jax import lax
from jax.experimental import pallas as pl
from jax.experimental.pallas import tpu as pltpu
from jax.sharding import PartitionSpec as P

BLK = 128
CAP = 4
BF16 = jnp.bfloat16
F32 = jnp.float32
WHOLE = pl.BlockSpec(memory_space=pltpu.VMEM)
SCALARS = pl.BlockSpec(memory_space=pltpu.SMEM)


def swap(x, axis, offset):
    size = lax.axis_size(axis)
    return lax.ppermute(x, axis, [(i, i ^ offset) for i in range(size)])


def shape(*dims, dtype=BF16):
    return jax.ShapeDtypeStruct(dims, dtype)


def column_offsets(n_col):
    return [n_col - 1, *range(1, n_col - 1)]


def nbytes(arrays):
    return sum(math.prod(a.shape) * jnp.dtype(a.dtype).itemsize for a in arrays)


def call(kernel, outs, operands, scratch=(), lists=()):
    held = nbytes(outs) + nbytes(scratch)
    operands = [pltpu.with_memory_space_constraint(x, pltpu.VMEM) for x in operands]
    return pl.pallas_call(
        kernel,
        out_shape=outs,
        in_specs=[SCALARS] * len(lists) + [WHOLE] * len(operands),
        out_specs=[WHOLE] * len(outs),
        scratch_shapes=[pltpu.VMEM(x.shape, x.dtype) for x in scratch],
        compiler_params=pltpu.CompilerParams(vmem_limit_bytes=held + (4 << 20)),
        cost_estimate=pl.CostEstimate(flops=0, bytes_accessed=0, transcendentals=0),
    )(*lists, *operands)


def part(index, size):
    return pl.ds(pl.multiple_of(index * size, size), size)


def later_kernel(x_ref, *refs):
    refs[-1][...] = x_ref[...]


def add_kernel(x_ref, y_ref, _, *outs):
    rows = outs[0].shape[0]
    for i, out in enumerate(outs):
        at = pl.ds(i * rows, rows)
        out[...] = (x_ref[at, :].astype(F32) + y_ref[at, :].astype(F32)).astype(out.dtype)


def stack_kernel(own, *refs):
    refs, out = refs[:-3], refs[-1]
    span = own.shape[0]
    half = span // 2
    out[:half, :] = own[half:, :]
    for i, ref in enumerate(refs):
        out[pl.ds(half + i * span, span), :] = ref[...]


def lists_kernel(held, spare, mine, theirs, _, which, code, which2, code2, made, count):
    r = lax.axis_index("row")
    made[...] = jnp.zeros_like(made)
    for refs in ((which, code), (which2, code2)):
        for i in range(refs[0].shape[0]):
            refs[0][i] = 0
            refs[1][i] = spare * held
    for t in range(count.shape[0]):
        count[t] = 0

    def place(k, _):
        for pulls, refs, at in (
            (mine, (which, code), 0),
            (theirs, (which2, code2), count.shape[0] // 2),
        ):
            t = pulls[0, k] ^ r

            @pl.when(t % 2 == 0)
            def _(pulls=pulls, refs=refs, at=at, t=t):
                chip = t // 2
                i = chip * CAP + count[at + chip]
                count[at + chip] += 1
                refs[0][i] = k
                refs[1][i] = pulls[2, k] * held + pulls[1, k]

        return 0

    lax.fori_loop(0, mine.shape[1], place, 0, unroll=True)


def aggregate_kernel(n_row, n_col, a_ref, own, other, *refs):
    near, (across, keep, send, x_ref) = refs[:-4], refs[-4:]
    span = own.shape[0]
    half = span // 2
    r, c = lax.axis_index("row"), lax.axis_index("col")
    x_ref[part(r, span), :] = own[...]
    x_ref[part(r ^ 1, span), :] = other[...]
    for i, ref in enumerate(near):
        t = 2 * (i + 1)
        x_ref[part(r ^ t, span), :] = ref[...]
        x_ref[part(r ^ t ^ 1, span), :] = across[pl.ds(half + i * span, span), :]
    for s in range(n_col):
        block = jnp.dot(a_ref[part(c ^ s, span), :], x_ref[...], preferred_element_type=F32)
        if s % 2:
            send[s // 2] = block.astype(BF16)
        else:
            keep[s // 2] = block


def halve_kernel(kept, received, keep, send):
    for i in range(kept.shape[0]):
        block = kept[i] + received[i].astype(F32)
        if i % 2:
            send[i // 2] = block.astype(BF16)
        else:
            keep[i // 2] = block


def project_kernel(kept, received, w_ref, _, projected, flipped):
    total = kept[0] + received[0].astype(F32)
    high = total.astype(BF16)
    low = (total - high.astype(F32)).astype(BF16)
    projected[...] = jnp.dot(high, w_ref[...], preferred_element_type=F32) + jnp.dot(
        low, w_ref[...], preferred_element_type=F32
    )
    flipped[...] = total.T.astype(BF16)


def add_pulls(pulls, held, code, tile_of, acc):
    half = held // 2
    for i, piece in pulls:
        slot = code[i] % held
        if len(piece) == 1:
            block = piece[0][part(slot, BLK), :]
        else:
            inside = part(slot % half, BLK)
            block = jnp.where(slot < half, piece[0][inside, :], piece[1][inside, :])
        rows = part(code[i] // held, BLK)
        acc[rows, :] += jnp.dot(tile_of(i), block, preferred_element_type=F32)


def slice_kernel(at, x_ref, out):
    out[...] = x_ref[pl.ds(at, out.shape[0]), :]


def pulls_of(chips, pieces):
    return [
        (i * CAP + m, piece)
        for i, piece in zip(chips, pieces, strict=True)
        for m in range(CAP)
    ]


def early_kernel(offsets, held, which, code, which2, code2, tiles, tiles2, *refs):
    pieces, (own, others) = [(ref,) for ref in refs[:-2]], refs[-2:]
    pulls = pulls_of(offsets, pieces)
    own[...] = jnp.zeros_like(own)
    others[...] = jnp.zeros_like(others)
    add_pulls(pulls, held, code2, lambda i: tiles2[which2[i]], others)
    add_pulls(pulls, held, code, lambda i: tiles[which[i]], own)


def others_kernel(offsets, held, count, which, code, acc_in, tiles, *refs):
    refs, outs, acc = refs[: -1 - count], refs[-1 - count : -1], refs[-1]
    pieces = list(zip(refs[::2], refs[1::2], strict=True))
    acc[...] = acc_in[...]
    add_pulls(pulls_of(offsets, pieces), held, code, lambda i: tiles[which[i]], acc)
    rows = outs[0].shape[0]
    for i, out in enumerate(outs):
        out[...] = acc[pl.ds(i * rows, rows), :].astype(BF16)


def own_kernel(offsets, held, which, code, acc_in, tiles, *refs):
    pieces, out = list(zip(refs[:-1:2], refs[1:-1:2], strict=True)), refs[-1]
    out[...] = acc_in[...]
    add_pulls(pulls_of(offsets, pieces), held, code, lambda i: tiles[which[i]], out)


def merge_kernel(n_col, projected, own, *refs):
    received, outs, acc = refs[:n_col], refs[n_col:-1], refs[-1]
    span = outs[0].shape[0]
    c = lax.axis_index("col")
    for i, ref in enumerate(received):
        rows = pl.ds(i * span, span)
        acc[rows, :] = own[rows, :] + ref[...].astype(F32)
    for s, out in enumerate(outs):
        block = acc[part(c ^ s, span), :]
        out[...] = block.astype(out.dtype) if s else block + projected[...]


def gradient_kernel(cotangent, kept, *refs):
    parts, (mixed_out, flipped) = refs[:-2], refs[-2:]
    mixed = kept[...]
    for ref in parts:
        mixed = mixed + ref[...].astype(F32)
    mixed_out[...] = mixed
    sigmoid_z = jax.nn.sigmoid(mixed)
    grad_pre = cotangent[...].astype(F32) * sigmoid_z * (1.0 + mixed * (1.0 - sigmoid_z))
    flipped[...] = grad_pre.T.astype(BF16)


def activate_kernel(mixed, kept, received, activated, total):
    activated[...] = (mixed[...] * jax.nn.sigmoid(mixed[...])).astype(BF16)
    total[...] = (kept[...] + received[...].astype(F32)).astype(BF16)


def scale_kernel(scale, *refs):
    refs, out = refs[:-1], refs[-1]
    count, rows = len(refs) // 2, refs[0].shape[0]
    core = lax.axis_index("row") % 2
    for i, ref in enumerate(refs):
        at = core if i < count else 1 - core
        out[part(at * count + i % count, rows), :] = ref[...].astype(F32) * scale


def nodes_kernel(w_ref, *refs):
    refs, out = refs[:-1], refs[-1]
    total = refs[0][...]
    for ref in refs[1:]:
        total = total + ref[...].astype(F32)
    out[...] = lax.dot_general(
        total.T.astype(BF16), w_ref[...], (((1,), (1,)), ((), ())), preferred_element_type=F32
    ).astype(BF16)


def weight_kernel(x_ref, g_ref, kept, given):
    half = x_ref.shape[0] // 2
    mine = lax.axis_index("row") % 2
    for out, core in ((kept, mine), (given, 1 - mine)):
        product = lax.dot_general(
            x_ref[part(core, half), :],
            g_ref[...],
            (((1,), (1,)), ((), ())),
            preferred_element_type=F32,
        )
        out[...] = product.astype(out.dtype)


def panel_kernel(offsets, *refs):
    pieces, out = refs[:-1], refs[-1]
    span = pieces[0].shape[1]
    c = lax.axis_index("col")
    for s, piece in zip(offsets, pieces, strict=True):
        out[:, part(c ^ s, span)] = piece[...]


def transposed_kernel(offsets, a_ref, g_ref, _, given, kept):
    span = kept.shape[2]
    r = lax.axis_index("row")
    for out, core in ((given, 1), (kept, 0)):
        for i, t in enumerate(offsets):
            columns = part(r ^ t ^ core, span)
            product = jnp.dot(g_ref[...], a_ref[:, columns], preferred_element_type=F32)
            out[i] = product.astype(out.dtype)


def tree_kernel(*refs):
    terms, out = [ref[...].astype(F32) for ref in refs[:-2]], refs[-1]
    while len(terms) > 1:
        terms = [a + b for a, b in zip(terms[::2], terms[1::2], strict=True)]
    out[...] = terms[0].astype(out.dtype)


def cores_kernel(places, kept, received, _, *outs):
    for i, out in zip(places, outs, strict=True):
        out[...] = (kept[i] + received[i].astype(F32)).astype(out.dtype)


def reduce_columns(keep, send):
    bit = 1
    while True:
        received = swap(send, "col", bit)
        count, span, hid = keep.shape
        if count == 1:
            return keep, received, send
        bit *= 2
        keep, send = call(
            halve_kernel,
            [shape(count // 2, span, hid, dtype=F32), shape(count // 2, span, hid)],
            [keep, received],
        )


def local(
    nodes, weight, adjacency, history, pull_owner, pull_slot, pull_target, hist_tiles, cotangent
):
    n_row, n_col = lax.axis_size("row"), lax.axis_size("col")
    span, hid = nodes.shape
    panel, columns = adjacency.shape
    row_count = panel // BLK
    chips = list(range(0, n_row, 2))
    offsets = column_offsets(n_col)

    pulls = jnp.stack([pull_owner[:, 0], pull_slot, pull_target])
    their_pulls = swap(pulls, "row", 1)
    tiles = swap(hist_tiles, "row", 1)

    beside = swap(nodes, "row", 1)
    near = [swap(nodes, "row", t) for t in chips[:0:-1]][::-1]
    (history,) = call(later_kernel, [shape(*history.shape)], [history, beside, tiles])
    blocks_held = history.shape[0] // BLK
    places = len(chips) * CAP
    which, code, which2, code2, made = pl.pallas_call(
        functools.partial(lists_kernel, blocks_held, row_count),
        out_shape=[shape(places, dtype=jnp.int32)] * 4 + [shape(8, 128, dtype=F32)],
        in_specs=[SCALARS] * 2 + [WHOLE],
        out_specs=[SCALARS] * 4 + [WHOLE],
        scratch_shapes=[pltpu.SMEM((n_row,), jnp.int32)],
        compiler_params=pltpu.CompilerParams(vmem_limit_bytes=4 << 20),
    )(pulls, their_pulls, history)

    (stacked,) = call(
        stack_kernel,
        [shape(span // 2 + len(near) * span, hid)],
        [nodes, *near, history, made],
    )
    across = swap(stacked, "row", 1)

    keep, send = call(
        functools.partial(aggregate_kernel, n_row, n_col),
        [shape(n_col // 2, span, hid, dtype=F32), shape(n_col // 2, span, hid)],
        [adjacency, nodes, beside, *near, across],
        [shape(columns, hid)],
    )
    keep, received, halved = reduce_columns(keep, send)

    middle = history.shape[0] // 2
    bits = [1 << b for b in range(1, n_row.bit_length() - 1)]
    past = {0: history, **{bit: swap(history, "row", bit) for bit in bits}}
    halves = []
    for at, order in ((0, bits), (middle, bits[::-1])):
        held = {}
        for bit in order:
            held.update({t ^ bit: swap(x, "row", bit) for t, x in list(held.items())})
            (held[bit],) = call(
                functools.partial(slice_kernel, at), [shape(middle, hid)], [past[bit]]
            )
        halves.append(held)
    early = [i for i, t in enumerate(chips) if t & (t - 1) == 0]
    early = [early[0], *early[:0:-1]]
    late = [i for i, t in enumerate(chips) if t & (t - 1)]
    forwarded = [held[chips[i]] for i in late for held in halves]

    spare = shape(panel + BLK, hid, dtype=F32)
    own_terms, terms = call(
        functools.partial(early_kernel, early, blocks_held),
        [spare, spare],
        [hist_tiles, tiles, *[past[chips[i]] for i in early]],
        lists=[which, code, which2, code2],
    )
    projected, summed = call(
        project_kernel, [shape(span, hid, dtype=F32), shape(hid, span)], [keep, received, weight, own_terms]
    )
    given = call(
        functools.partial(others_kernel, late, blocks_held, n_col),
        [shape(span, hid)] * n_col,
        [terms, tiles, *forwarded],
        [spare],
        [which2, code2],
    )
    received = [swap(x, "row", 1) for x in given]
    (terms,) = call(
        functools.partial(own_kernel, late, blocks_held),
        [spare],
        [own_terms, hist_tiles, *forwarded],
        lists=[which, code],
    )
    keep, *sends = call(
        functools.partial(merge_kernel, n_col),
        [shape(span, hid, dtype=BF16 if s else F32) for s in range(n_col)],
        [projected, terms, *received],
        [shape(panel, hid, dtype=F32)],
    )
    mixed, flipped = call(
        gradient_kernel,
        [shape(span, hid, dtype=F32), shape(hid, span)],
        [cotangent, keep, *[swap(sends[s - 1], "col", s) for s in offsets]],
    )

    pieces = [swap(flipped, "col", s) if s else flipped for s in [*offsets, 0]]
    kept, given = call(
        weight_kernel,
        [shape(hid // 2, hid, dtype=F32), shape(hid // 2, hid)],
        [summed, flipped],
    )
    activated, kept = call(
        activate_kernel,
        [shape(span, hid), shape(hid // 2, hid)],
        [mixed, kept, swap(given, "row", 1)],
    )
    gradients = call(
        functools.partial(panel_kernel, [*offsets, 0]), [shape(hid, panel)], pieces
    )[0]
    (halfway,) = call(
        tree_kernel,
        [shape(hid // 2, hid)],
        [*[swap(kept, "row", t) if t else kept for t in chips], gradients],
    )

    given, kept = call(
        functools.partial(transposed_kernel, chips),
        [shape(len(chips), hid, span, dtype=dtype) for dtype in (BF16, F32)],
        [adjacency, gradients, halfway],
    )
    received = swap(given, "row", 1)
    arrived, token = {}, given
    for places in (list(range(1, len(chips))), [0]):
        sums = call(
            functools.partial(cores_kernel, places),
            [shape(hid, span, dtype=BF16 if i else F32) for i in places],
            [kept, received, token],
        )
        for i, x in zip(places, sums, strict=True):
            arrived[i] = swap(x, "row", chips[i]) if i else x
        if token is given:
            beside = swap(halfway, "col", 1)
            (token,) = call(add_kernel, [shape(*halfway.shape)], [halfway, beside, sums[0]])
    halfway = token
    (grad_nodes,) = call(
        nodes_kernel, [shape(span, hid)], [weight, *[arrived[i] for i in range(len(chips))]]
    )

    halfway = [halfway]
    for bit in [1 << b for b in range(1, n_col.bit_length() - 1)]:
        received = swap(halfway[0], "col", bit)
        count = 2 if 2 * bit == n_col else 1
        halfway = call(
            add_kernel,
            [shape(hid // 2 // count, hid)] * count,
            [halfway[0], received, arrived[len(chips) - 1]],
        )
    scale = 1.0 / math.sqrt(span * n_row * n_col)
    (grad_weight,) = call(
        functools.partial(scale_kernel, scale),
        [shape(hid, hid, dtype=F32)],
        [*halfway, *[swap(x, "row", 1) for x in halfway]],
    )
    return (activated, grad_nodes, grad_weight)


def solution(mesh):
    return jax.shard_map(
        local,
        mesh=mesh,
        in_specs=(
            P(("row", "col"), None),
            P(),
            P("row", "col"),
            P(("row", "col"), None),
            P(("row", "col"), None),
            P(("row", "col")),
            P(("row", "col")),
            P(("row", "col"), None, None),
            P(("row", "col"), None),
        ),
        out_specs=(P(("row", "col"), None), P(("row", "col"), None), P()),
        check_vma=False,
    )
```
